256 devices in a mesh: hier: 4 (over x), row: 64 (over z, y, core).
Axes of the slice: x: 4, y: 4, z: 8, core: 2. Of those that a mesh axis runs over, the one named last changes fastest.
Arguments:
- rho: float32 [64, 2, 1024, 1024], P('hier', None, 'row'), may hold values from -6 to 6
- incr: float32 [64, 2, 1024, 1024], P('hier', None, 'row'), may hold values from -6 to 6
- accum: float32 [64, 2, 1024, 1024], P('hier', None, 'row'), may hold values from -6 to 6
- ham: float32 [1024, 1024], P('row'), as said below
- modes: float32 [8, 1024], replicated, may hold values from -4 to 4
- coeff: float32 [2, 8], replicated, may hold values from 0.2 to 1
- damping: float32 [64], P('hier'), may hold values from 0.1 to 3
- links: int32 [64, 4], replicated, may hold values from 0 to 63, as said below
- bath: int32 [64, 4], replicated, may hold values from 0 to 7
- kinds: int32 [64, 4], replicated, may hold values from 0 to 2
Outputs:
- deriv: float32 [64, 2, 1024, 1024], P('hier', None, 'row')
- accum_new: float32 [64, 2, 1024, 1024], P('hier', None, 'row')
The draws below stay inside these ranges and needn't reach their ends.
Inputs may be any that keep to these rules, and one draw needn't show every extreme that they name: ham is exactly symmetric. `links`: an unused slot names its own matrix. For every two different hierarchy groups g and h (matrices g * 16 to (g + 1) * 16 - 1 form group g), the used slots of g's matrices name exactly 4 distinct matrices of group h.
All inputs are finite; a program needn't handle non-finite values.
Results may differ from the reference program's by a relative error of at most 0.0003.
Values sent between devices are 32-bit elements; how exact they have to be, the bound alone decides.
A program may use at most 128 MiB of HBM per device.

```python
import math
import jax
import jax.numpy as jnp
from jax import lax

N = 1024
BATH = 8
SLOTS = 4
AUX_GRP = 16
AUX = 64
CAP = 4


def couplings(key):
    groups = AUX // AUX_GRP
    subkeys = jax.random.split(key, 7)
    aux_ids = jnp.arange(AUX, dtype=jnp.int32)[:, None]
    slot_ids = jnp.arange(SLOTS, dtype=jnp.int32)[None, :]
    owner_group = aux_ids // AUX_GRP
    inner_slot = aux_ids % AUX_GRP
    rotation = jax.random.randint(subkeys[0], (groups, groups), 0, AUX_GRP)
    active = jax.random.randint(subkeys[1], (AUX, SLOTS), 0, groups) <= owner_group
    remote_use = jax.random.randint(subkeys[2], (AUX, SLOTS), 0, 2) == 1
    offset = jax.random.randint(subkeys[3], (AUX, SLOTS), 1, groups)
    target = (owner_group + offset) % groups
    chosen = jax.random.randint(subkeys[4], (AUX, SLOTS), 0, CAP)
    near_pick = (inner_slot + jax.random.randint(subkeys[5], (AUX, SLOTS), 1, AUX_GRP)) % AUX_GRP
    position = slot_ids * AUX_GRP + inner_slot
    forced = position < (groups - 1) * CAP
    target = jnp.where(forced, (owner_group + 1 + position // CAP) % groups, target)
    chosen = jnp.where(forced, position % CAP, chosen)
    remote_use = remote_use | forced
    active = active | forced
    remote = target * AUX_GRP + (rotation[owner_group, target] + chosen) % AUX_GRP
    local_ids = owner_group * AUX_GRP + near_pick
    own_ids = jnp.broadcast_to(aux_ids, (AUX, SLOTS))
    link_ids = jnp.where(active, jnp.where(remote_use, remote, local_ids), own_ids).astype(jnp.int32)
    kind_ids = jnp.where(active, jax.random.randint(subkeys[6], (AUX, SLOTS), 1, 3), 0).astype(jnp.int32)
    return (link_ids, kind_ids)


def draw_links(key, part):
    link_ids, kind_ids = couplings(key)
    return link_ids


def draw_kinds(key, part):
    link_ids, kind_ids = couplings(key)
    return kind_ids


def draw_ham(key, part):
    key = jax.random.fold_in(key, 11)
    first, second = jax.random.split(key)
    halves = jax.random.normal(first, (N, N), jnp.float32) / jnp.sqrt(2.0 * N)
    energies = jax.random.uniform(second, (N,), jnp.float32, -1.0, 1.0)
    return (halves + halves.T + jnp.diag(energies)).astype(jnp.float32)


def place_ends(array, stream_key, low, top_value):
    longest = array.shape.index(max(array.shape))
    spots = []
    for shift in (0, 1):
        where = [jax.random.randint(jax.random.fold_in(stream_key, axis), (), 0, length) for axis, length in enumerate(array.shape)]
        where[longest] = (where[longest] + shift) % array.shape[longest]
        spots.append(tuple(where))
    return array.at[spots[0]].set(low).at[spots[1]].set(top_value)


def shard_levels(own_key, shape, pieces, least, top_value):
    loudness, own = 1.0, jax.random.fold_in(own_key, 6)
    for dim, shards_of in pieces:
        steps = jnp.exp(jax.random.uniform(jax.random.fold_in(own, dim), (shards_of,), jnp.float32, least / len(pieces), top_value / len(pieces)))
        loudness = loudness * jnp.repeat(steps, shape[dim] // shards_of).reshape([-1 if axis == dim else 1 for axis in range(len(shape))])
    return loudness


def scatter_about(rng, extent, scale, limit, cuts=(), kind=jnp.bfloat16):
    entries = jax.random.normal(rng, extent, jnp.float32) * scale
    if len(cuts) > 0:
        entries = shard_levels(rng, extent, cuts, -0.22, 0.18) * entries
    return jnp.clip(entries, min=-limit, max=limit).astype(kind)


def setup_inputs(seed: int = 0) -> dict:
    arg_keys = jax.random.split(jax.random.key(seed), 11)
    return {
        "rho": scatter_about(arg_keys[0], (AUX, 2, N, N), 1.0, 6.0, ((0, 4), (2, 64)), jnp.float32),
        "incr": scatter_about(arg_keys[1], (AUX, 2, N, N), 1.0, 6.0, ((0, 4), (2, 64)), jnp.float32),
        "accum": scatter_about(arg_keys[2], (AUX, 2, N, N), 1.0, 6.0, ((0, 4), (2, 64)), jnp.float32),
        "ham": draw_ham(jax.random.fold_in(arg_keys[10], 71), 0),
        "modes": scatter_about(arg_keys[4], (BATH, N), 1.0, 4.0, (), jnp.float32),
        "coeff": jnp.clip(jax.random.uniform(arg_keys[5], (2, BATH), jnp.float32, 0.2, 1.0), 0.2, 1.0),
        "damping": jnp.clip(jnp.exp(math.log(3.0) - 3.4011974 * jax.random.uniform(arg_keys[6], (AUX,), jnp.float32) ** shard_levels(arg_keys[6], (AUX,), ((0, 4),), -0.2, 0.2)), 0.1, 3.0),
        "links": draw_links(jax.random.fold_in(arg_keys[10], 71), 0),
        "bath": place_ends(jax.random.randint(arg_keys[8], (AUX, SLOTS), 0, BATH), jax.random.fold_in(arg_keys[8], 1), 0, BATH - 1).astype(jnp.int32),
        "kinds": draw_kinds(jax.random.fold_in(arg_keys[10], 71), 0),
    }


half_step = 0.1
third_step = 0.2 / 3.0


def reference(rho, incr, accum, ham, modes, coeff, damping, links, bath, kinds):
    section_arg = rho + half_step * incr

    def one_aux(aux_id):
        matrix = section_arg[aux_id]
        commutator = jnp.matmul(ham, matrix, precision=lax.Precision.HIGHEST) - jnp.matmul(matrix, ham, precision=lax.Precision.HIGHEST)
        result = jnp.stack([commutator[1], -commutator[0]]) - damping[aux_id] * matrix
        for slot in range(SLOTS):
            neighbour = section_arg[links[aux_id, slot]]
            bath_now = bath[aux_id, slot]
            weights = modes[bath_now]
            kind_now = kinds[aux_id, slot]
            raising = (kind_now == 1).astype(jnp.float32)
            lowering = (kind_now == 2).astype(jnp.float32)
            direct = raising + lowering * coeff[0, bath_now]
            mixing = lowering * coeff[1, bath_now]
            gap_field = weights[:, None] - weights[None, :]
            sum_field = weights[:, None] + weights[None, :]
            real_term = direct * gap_field * neighbour[1] + mixing * sum_field * neighbour[0]
            imag_term = -(direct * gap_field * neighbour[0]) + mixing * sum_field * neighbour[1]
            result = result + jnp.stack([real_term, imag_term])
        return result

    deriv = lax.map(one_aux, jnp.arange(AUX, dtype=jnp.int32))
    return deriv, accum + third_step * deriv
```

```python
import jax
import jax.numpy as jnp
from jax import lax
from jax.experimental import pallas as pl
from jax.experimental.pallas import tpu as pltpu
from jax.sharding import PartitionSpec as P

half_step = 0.1
third_step = 0.2 / 3.0

MESH = pl.DeviceIdType.MESH
GROUPS = 4
ZS = 8
YS = 4
YC = 8
OWN = 16
CAP = 4
MATS = 32
ROWS = 16
N = 1024
BATH = 8
SLOTS = 4
CHUNKS = 4
WIDE = N // CHUNKS
HALF = WIDE // 2
QUART = N // GROUPS
TILE = 256


def split(x):
    hi = x.astype(jnp.bfloat16)
    return hi, (x - hi.astype(jnp.float32)).astype(jnp.bfloat16)


def dot(a, b):
    return jnp.dot(a, b, preferred_element_type=jnp.float32)


def sorted_links(links_vec, rows_of, target):
    block = links_vec[pl.ds(pl.multiple_of(rows_of * OWN, OWN), OWN), :]
    low = target * OWN
    found, last = [], low - 1
    for _ in range(CAP):
        inside = (block > last) & (block < low + OWN)
        last = jnp.minimum(jnp.min(jnp.where(inside, block, low + OWN - 1)), low + OWN - 1)
        found.append(last)
    return found


def kernel(
    rho, incr, ham, modes, links_vec, coeff, damping, links, bath, kinds,
    deriv,
    panels, rho_buf, incr_buf, ham_buf, ham_hi, ham_lo, z_in, y_in, right_cat, left, y_back, z_back,
    acc, pool, picked, gap, total,
    load_sem, h1_send, h1_recv, h2_send, h2_recv, h3_send, h3_recv, h4_send, h4_recv,
    zi_send, zi_recv, yi_send, yi_recv, yb_send, yb_recv, zb_send, zb_recv, pick_send, pick_recv, out_sem,
):
    h = lax.axis_index("hier")
    r = lax.axis_index("row")
    z = r // YC
    yc = r % YC
    y = yc // 2
    c = yc % 2

    def remote(src, dst, send, recv, group, row):
        return pltpu.make_async_remote_copy(
            src_ref=src, dst_ref=dst, send_sem=send, recv_sem=recv,
            device_id=(group, row), device_id_type=MESH,
        )

    def wait_bytes(ref, sem):
        pltpu.make_async_copy(ref, ref, sem).wait()

    def other_z(k):
        there = (z + k) % ZS
        return there, there * YC + yc

    def other_yc(k):
        there = (yc + k) % YC
        return there, z * YC + there

    def each(first, last, body):
        def step(k, carry):
            body(k)
            return carry

        lax.fori_loop(first, last, step, 0)

    load_rho = pltpu.make_async_copy(rho, rho_buf, load_sem.at[0])
    load_incr = pltpu.make_async_copy(incr, incr_buf, load_sem.at[1])
    load_rho.start()
    load_incr.start()
    barrier = pltpu.get_barrier_semaphore()

    def greet(group, row):
        pl.semaphore_signal(barrier, inc=1, device_id=(group, row), device_id_type=MESH)

    each(1, ZS, lambda k: greet(h, other_z(k)[1]))
    each(1, YC, lambda k: greet(h, other_yc(k)[1]))
    each(1, GROUPS, lambda k: greet((h + k) % GROUPS, r))

    load_rho.wait()
    load_incr.wait()

    def make_panel(m):
        value = rho_buf[m] + half_step * incr_buf[m]
        panels[m] = value
        pool[m] = value

    each(0, MATS, make_panel)
    pl.semaphore_wait(barrier, ZS - 1 + YC - 1 + GROUPS - 1)

    ham_own = ham.at[:, pl.ds(pl.multiple_of(h * QUART, QUART), QUART)]
    h1_local = pltpu.make_async_copy(ham_own, ham_buf.at[h, c, z, y], h1_recv)
    h1_local.start()
    each(1, ZS, lambda k: remote(ham_own, ham_buf.at[h, c, z, y], h1_send, h1_recv, h, other_z(k)[1]).start())

    for j in range(CHUNKS):
        cols = pl.ds(j * WIDE, WIDE)

        def send_z(k, j=j, cols=cols):
            there, row = other_z(k)
            remote(
                panels.at[pl.ds(there * YS, YS), :, cols], z_in.at[j, z], zi_send.at[j], zi_recv.at[j], h, row
            ).start()

        pltpu.make_async_copy(panels.at[pl.ds(z * YS, YS), :, cols], z_in.at[j, z], zi_recv.at[j]).start()
        each(1, ZS, send_z)

    wait_bytes(ham_buf.at[h, c, :, y], h1_recv)
    own_y = ham_buf.at[h, c, :, y]
    each(1, YS, lambda k: remote(own_y, own_y, h2_send, h2_recv, h, z * YC + (y + k) % YS * 2 + c).start())

    for d in range(1, GROUPS):
        chosen = sorted_links(links_vec, (h + d) % GROUPS, h)
        for i in range(CAP):
            place = (chosen[i] - h * OWN) * 2
            picked[d - 1, 2 * i] = panels[place]
            picked[d - 1, 2 * i + 1] = panels[place + 1]

    wait_bytes(ham_buf.at[h, c, :, pl.ds(0, YS - 1)], h2_recv)
    for d in (1, 3, 2):
        remote(
            ham_buf.at[h, c], ham_buf.at[h, c], h3_send.at[d - 1], h3_recv.at[d - 1], (h + d) % GROUPS, r
        ).start()

    def to_core(d):
        quarter = ham_buf.at[(h + GROUPS - d) % GROUPS, c]
        return remote(quarter, quarter, h4_send.at[d], h4_recv.at[d], h, r - c + 1 - c)

    to_core(0).start()
    for d in (1, 3, 2):
        remote(
            picked.at[d - 1], pool.at[pl.ds(MATS + (d - 1) * 2 * CAP, 2 * CAP)],
            pick_send.at[d - 1], pick_recv.at[d - 1], (h + d) % GROUPS, r,
        ).start()

    def forward_in(j):
        wait_bytes(z_in.at[j], zi_recv.at[j])

        def send_y(k):
            there, row = other_yc(k)
            remote(
                z_in.at[j, :, there // 2, :, pl.ds(pl.multiple_of(there % 2 * HALF, HALF), HALF)],
                y_in.at[j, :, yc], yi_send.at[j], yi_recv.at[j], h, row,
            ).start()

        pltpu.make_async_copy(
            z_in.at[j, :, y, :, pl.ds(pl.multiple_of(c * HALF, HALF), HALF)], y_in.at[j, :, yc], yi_recv.at[j]
        ).start()
        each(1, YC, send_y)

    def take_ham(d):
        q = (h + GROUPS - d) % GROUPS
        wait_bytes(ham_buf.at[q, 1 - c], h4_recv.at[d])
        cols = pl.ds(pl.multiple_of(q * QUART, QUART), QUART)

        def part(k):
            zz, yy = k // YS, k % YS
            for cc in range(2):
                hi, lo = split(ham_buf[q, cc, zz, yy])
                rows = pl.ds(pl.multiple_of((k * 2 + cc) * ROWS, ROWS), ROWS)
                ham_hi[rows, cols] = hi
                ham_lo[rows, cols] = lo

        each(0, ZS * YS, part)

    def multiply_left(j):
        wait_bytes(y_in.at[j], yi_recv.at[j])

        def cut(k):
            hi, lo = split(y_in[j, k].reshape(YC * ROWS, HALF))
            rows = pl.ds(pl.multiple_of(k * YC * ROWS, YC * ROWS), YC * ROWS)
            right_cat[rows, 0:HALF] = hi
            right_cat[rows, HALF:WIDE] = lo

        each(0, ZS, cut)

        def tile(k):
            rows = pl.ds(pl.multiple_of(k * TILE, TILE), TILE)
            both = dot(ham_hi[rows, :], right_cat[...])
            value = both[:, HALF:] + dot(ham_lo[rows, :], right_cat[:, 0:HALF]) + both[:, :HALF]
            left[j, pl.ds(k * 2, 2)] = value.reshape(2, YC, ROWS, HALF)

        each(0, N // TILE, tile)

        def send_y(k):
            there, row = other_yc(k)
            remote(
                left.at[j, :, there], y_back.at[j, :, y, :, pl.ds(pl.multiple_of(c * HALF, HALF), HALF)],
                yb_send.at[j], yb_recv.at[j], h, row,
            ).start()

        pltpu.make_async_copy(
            left.at[j, :, yc], y_back.at[j, :, y, :, pl.ds(pl.multiple_of(c * HALF, HALF), HALF)], yb_recv.at[j]
        ).start()
        each(1, YC, send_y)

    def forward_back(j):
        wait_bytes(y_back.at[j], yb_recv.at[j])

        def send_z(k):
            there, row = other_z(k)
            remote(
                y_back.at[j, there], z_back.at[j, pl.ds(z * YS, YS)], zb_send.at[j], zb_recv.at[j], h, row
            ).start()

        pltpu.make_async_copy(y_back.at[j, z], z_back.at[j, pl.ds(z * YS, YS)], zb_recv.at[j]).start()
        each(1, ZS, send_z)

    def multiply_right(k):
        rows = pl.ds(k * (TILE // ROWS), TILE // ROWS)
        hi, lo = split(panels[rows].reshape(TILE, N))

        def columns(q):
            cols = pl.ds(pl.multiple_of(q * TILE, TILE), TILE)
            top = ham_hi[:, cols]
            value = dot(hi, ham_lo[:, cols]) + dot(lo, top) + dot(hi, top)
            value = value.reshape(TILE // ROWS // 2, 2, ROWS, TILE)
            pairs = pl.ds(k * (TILE // ROWS // 2), TILE // ROWS // 2)
            acc[pairs, 0, :, cols] = acc[pairs, 0, :, cols] - value[:, 1]
            acc[pairs, 1, :, cols] = acc[pairs, 1, :, cols] + value[:, 0]

        each(0, N // TILE, columns)

    def decay(a):
        rate = damping[a]
        acc[a, 0] = -(rate * panels[2 * a])
        acc[a, 1] = -(rate * panels[2 * a + 1])

    each(0, OWN, decay)

    lane = lax.broadcasted_iota(jnp.int32, (ROWS, N), 1)
    diagonal = lane == lax.broadcasted_iota(jnp.int32, (ROWS, N), 0) + r * ROWS
    for k in range(BATH):
        columns = jnp.broadcast_to(modes[k : k + 1, :], (ROWS, N))
        row_part = jnp.sum(jnp.where(diagonal, columns, 0.0), axis=1, keepdims=True)
        gap[k] = row_part - columns
        total[k] = row_part + columns

    forward_in(0)
    forward_in(1)
    take_ham(0)
    for d in (1, 3, 2):
        wait_bytes(ham_buf.at[(h + GROUPS - d) % GROUPS, c], h3_recv.at[d - 1])
        to_core(d).start()
    forward_in(2)
    for d in (1, 3, 2):
        take_ham(d)
    multiply_left(0)
    multiply_left(1)
    forward_back(0)
    forward_in(3)
    forward_back(1)
    multiply_left(2)
    forward_back(2)
    multiply_left(3)
    forward_back(3)
    each(0, MATS * ROWS // TILE, multiply_right)

    for d in range(1, GROUPS):
        wait_bytes(pool.at[pl.ds(MATS + (d - 1) * 2 * CAP, 2 * CAP)], pick_recv.at[d - 1])
    names = []
    for d in range(1, GROUPS):
        names += sorted_links(links_vec, h, (h + GROUPS - d) % GROUPS)

    def couple(a):
        real, imag = acc[a, 0], acc[a, 1]
        for slot in range(SLOTS):
            link = links[h * OWN + a, slot]
            mode = bath[h * OWN + a, slot]
            kind = kinds[h * OWN + a, slot]
            place = link - h * OWN
            for i, name in enumerate(names):
                place = jnp.where(link == name, OWN + i, place)
            direct = jnp.where(kind == 1, 1.0, jnp.where(kind == 2, coeff[0, mode], 0.0))
            mixing = jnp.where(kind == 2, coeff[1, mode], 0.0)
            first, second = pool[2 * place], pool[2 * place + 1]
            across = direct * gap[mode]
            along = mixing * total[mode]
            real = real + (across * second + along * first)
            imag = imag + (along * second - across * first)
        acc[a, 0], acc[a, 1] = real, imag

    each(0, OWN, couple)

    stores = []
    for j in range(CHUNKS):
        cols = pl.ds(j * WIDE, WIDE)
        wait_bytes(z_back.at[j], zb_recv.at[j])

        def finish(a, j=j, cols=cols):
            acc[a, 0, :, cols] = acc[a, 0, :, cols] + z_back[j, 2 * a + 1]
            acc[a, 1, :, cols] = acc[a, 1, :, cols] - z_back[j, 2 * a]

        each(0, OWN, finish)
        store = pltpu.make_async_copy(acc.at[:, :, :, cols], deriv.at[:, :, :, cols], out_sem.at[j])
        store.start()
        stores.append(store)

    wait_bytes(ham_buf.at[0, 0, pl.ds(0, ZS - 1), 0], h1_send)
    wait_bytes(ham_buf.at[0, 0, :, pl.ds(0, YS - 1)], h2_send)
    for d in range(GROUPS):
        wait_bytes(ham_buf.at[0, 0], h4_send.at[d])
    for d in range(1, GROUPS):
        wait_bytes(ham_buf.at[0, 0], h3_send.at[d - 1])
        wait_bytes(picked.at[0], pick_send.at[d - 1])
    for j in range(CHUNKS):
        wait_bytes(z_in.at[0, pl.ds(0, ZS - 1)], zi_send.at[j])
        wait_bytes(y_in.at[0, :, pl.ds(0, YC - 1)], yi_send.at[j])
        wait_bytes(left.at[0, :, pl.ds(0, YC - 1)], yb_send.at[j])
        wait_bytes(y_back.at[0, pl.ds(0, ZS - 1)], zb_send.at[j])
    for store in stores:
        store.wait()


def section(rho, incr, ham, modes, coeff, damping, links, bath, kinds):
    vmem = pl.BlockSpec(memory_space=pltpu.VMEM)
    smem = pl.BlockSpec(memory_space=pltpu.SMEM)
    any_space = pl.BlockSpec(memory_space=pl.ANY)
    f32, bf16 = jnp.float32, jnp.bfloat16
    dma = pltpu.SemaphoreType.DMA
    four = (CHUNKS,)
    return pl.pallas_call(
        kernel,
        out_shape=jax.ShapeDtypeStruct((OWN, 2, ROWS, N), f32),
        in_specs=[any_space, any_space, vmem, vmem, vmem, smem, smem, smem, smem, smem],
        out_specs=any_space,
        scratch_shapes=[
            pltpu.VMEM((MATS, ROWS, N), f32),
            pltpu.VMEM((MATS, ROWS, N), f32),
            pltpu.VMEM((MATS, ROWS, N), f32),
            pltpu.VMEM((GROUPS, 2, ZS, YS, ROWS, QUART), f32),
            pltpu.VMEM((N, N), bf16),
            pltpu.VMEM((N, N), bf16),
            pltpu.VMEM((CHUNKS, ZS, YS, ROWS, WIDE), f32),
            pltpu.VMEM((CHUNKS, ZS, YC, ROWS, HALF), f32),
            pltpu.VMEM((N, WIDE), bf16),
            pltpu.VMEM((CHUNKS, ZS, YC, ROWS, HALF), f32),
            pltpu.VMEM((CHUNKS, ZS, YS, ROWS, WIDE), f32),
            pltpu.VMEM((CHUNKS, MATS, ROWS, WIDE), f32),
            pltpu.VMEM((OWN, 2, ROWS, N), f32),
            pltpu.VMEM((MATS + (GROUPS - 1) * 2 * CAP, ROWS, N), f32),
            pltpu.VMEM((GROUPS - 1, 2 * CAP, ROWS, N), f32),
            pltpu.VMEM((BATH, ROWS, N), f32),
            pltpu.VMEM((BATH, ROWS, N), f32),
            dma((2,)),
            dma, dma, dma, dma,
            dma((3,)), dma((3,)), dma(four), dma(four),
            dma(four), dma(four), dma(four), dma(four),
            dma(four), dma(four), dma(four), dma(four),
            dma((3,)), dma((3,)),
            dma(four),
        ],
        compiler_params=pltpu.CompilerParams(
            collective_id=0, has_side_effects=True, vmem_limit_bytes=48 * 1024 * 1024
        ),
        cost_estimate=pl.CostEstimate(flops=6 * 2**30, bytes_accessed=6 * 2**20, transcendentals=0),
        name="section",
    )(rho, incr, ham, modes, links, coeff, damping, links, bath, kinds)


def local(rho, incr, accum, ham, modes, coeff, damping, links, bath, kinds):
    shape = rho.shape
    deriv = section(
        rho.reshape(MATS, ROWS, N), incr.reshape(MATS, ROWS, N), ham, modes, coeff, damping, links, bath, kinds
    ).reshape(shape)
    return (deriv, accum + third_step * deriv)


def solution(mesh):
    in_specs = (
        P("hier", None, "row", None),
        P("hier", None, "row", None),
        P("hier", None, "row", None),
        P("row", None),
        P(),
        P(),
        P("hier"),
        P(),
        P(),
        P(),
    )
    out_specs = (P("hier", None, "row", None), P("hier", None, "row", None))
    return jax.shard_map(local, mesh=mesh, in_specs=in_specs, out_specs=out_specs, check_vma=False)
```

```python
import jax
import jax.numpy as jnp
from jax import lax
from jax.experimental import pallas as pl
from jax.experimental.pallas import tpu as pltpu
from jax.sharding import PartitionSpec as P

half_step = 0.1
third_step = 0.2 / 3.0

MESH = pl.DeviceIdType.MESH
GROUPS = 4
ZS = 8
YS = 4
YC = 8
OWN = 16
CAP = 4
MATS = 32
ROWS = 16
N = 1024
BATH = 8
SLOTS = 4
CHUNKS = 4
WIDE = N // CHUNKS
HALF = WIDE // 2
QUART = N // GROUPS
TILE = 256


def split(x):
    hi = x.astype(jnp.bfloat16)
    return hi, (x - hi.astype(jnp.float32)).astype(jnp.bfloat16)


def dot(a, b):
    return jnp.dot(a, b, preferred_element_type=jnp.float32)


def sorted_links(links_vec, rows_of, target):
    block = links_vec[...]
    member = lax.broadcasted_iota(jnp.int32, block.shape, 1) - rows_of * OWN
    mine = (member >= 0) & (member < OWN)
    low = target * OWN
    found, last = [], low - 1
    for _ in range(CAP):
        inside = mine & (block > last) & (block < low + OWN)
        last = jnp.minimum(jnp.min(jnp.where(inside, block, low + OWN - 1)), low + OWN - 1)
        found.append(last)
    return found


def kernel(
    rho, incr, accum, ham_hbm, modes_hbm, coeff_hbm, damping_hbm, links_hbm, bath_hbm, kinds_hbm,
    acc, new,
    ham, modes, coeff, damping, links_vec, links, bath, kinds,
    panels, rho_buf, incr_buf, ham_buf, ham_hi, ham_lo, z_in, y_in, right_cat, left, y_back, z_back,
    pool, picked, gap, total,
    rho_sem, incr_sem, load_sem, h1_send, h1_recv, h2_send, h2_recv, h3_send, h3_recv, h4_send, h4_recv,
    zi_send, zi_recv, yi_send, yi_recv, yb_send, yb_recv, zb_send, zb_recv, pick_send, pick_recv,
):
    h = lax.axis_index("hier")
    r = lax.axis_index("row")
    z = r // YC
    yc = r % YC
    y = yc // 2
    c = yc % 2

    def remote(src, dst, send, recv, group, row):
        return pltpu.make_async_remote_copy(
            src_ref=src, dst_ref=dst, send_sem=send, recv_sem=recv,
            device_id=(group, row), device_id_type=MESH,
        )

    def wait_bytes(ref, sem):
        pltpu.make_async_copy(ref, ref, sem).wait()

    def other_z(k):
        there = (z + k) % ZS
        return there, there * YC + yc

    def other_yc(k):
        there = (yc + k) % YC
        return there, z * YC + there

    def each(first, last, body):
        def step(k, carry):
            body(k)
            return carry

        lax.fori_loop(first, last, step, 0)

    def load_panel(j):
        part = (slice(None), slice(None), pl.ds(j * WIDE, WIDE))
        return (
            pltpu.make_async_copy(rho.at[part], rho_buf.at[part], rho_sem.at[j]),
            pltpu.make_async_copy(incr.at[part], incr_buf.at[part], incr_sem.at[j]),
        )

    pairs = [
        (ham_hbm, ham), (modes_hbm, modes), (coeff_hbm, coeff), (damping_hbm, damping), (links_hbm, links_vec),
        (links_hbm, links), (bath_hbm, bath), (kinds_hbm, kinds), (accum, new),
    ]
    loads = [pltpu.make_async_copy(src, dst, load_sem.at[i]) for i, (src, dst) in enumerate(pairs)]
    for load in load_panel(0):
        load.start()
    loads[0].start()
    barrier = pltpu.get_barrier_semaphore()

    def greet(group, row):
        pl.semaphore_signal(barrier, inc=1, device_id=(group, row), device_id_type=MESH)

    each(1, ZS, lambda k: greet(h, other_z(k)[1]))
    each(1, YC, lambda k: greet(h, other_yc(k)[1]))
    each(1, GROUPS, lambda k: greet((h + k) % GROUPS, r))

    for j in range(1, CHUNKS):
        for load in load_panel(j):
            load.start()
    for load in loads[1:]:
        load.start()

    def make_panels(j):
        for load in load_panel(j):
            load.wait()
        cols = pl.ds(j * WIDE, WIDE)

        def make(m):
            part = pl.ds(m * 8, 8)
            panels[part, :, cols] = rho_buf[part, :, cols] + half_step * incr_buf[part, :, cols]

        each(0, MATS // 8, make)

    make_panels(0)
    loads[0].wait()
    pl.semaphore_wait(barrier, ZS - 1 + YC - 1 + GROUPS - 1)

    ham_own = ham.at[:, pl.ds(pl.multiple_of(h * QUART, QUART), QUART)]
    h1_local = pltpu.make_async_copy(ham_own, ham_buf.at[h, c, z, y], h1_recv)
    h1_local.start()
    each(1, ZS, lambda k: remote(ham_own, ham_buf.at[h, c, z, y], h1_send, h1_recv, h, other_z(k)[1]).start())

    def start_chunk(j):
        if j == 1:
            make_panels(j)
        cols = pl.ds(j * WIDE, WIDE)

        def send_z(k):
            there, row = other_z(k)
            remote(
                panels.at[pl.ds(there * YS, YS), :, cols], z_in.at[j, z], zi_send.at[j], zi_recv.at[j], h, row
            ).start()

        pltpu.make_async_copy(panels.at[pl.ds(z * YS, YS), :, cols], z_in.at[j, z], zi_recv.at[j]).start()
        each(1, ZS, send_z)

    def sent_chunk(j):
        wait_bytes(z_in.at[0, pl.ds(0, ZS - 1)], zi_send.at[j])

    start_chunk(0)
    start_chunk(1)

    wait_bytes(ham_buf.at[h, c, :, y], h1_recv)
    low, high = pl.ds(0, ZS // 2), pl.ds(ZS // 2, ZS // 2)

    def y_row(k):
        return z * YC + (y + k) % YS * 2 + c

    for k in (1, 3, 2):
        part = ham_buf.at[h, c, low, y]
        remote(part, part, h2_send.at[0], h2_recv.at[0], h, y_row(k)).start()
        part = ham_buf.at[h, c, high, y]
        remote(part, part, h2_send.at[1], h2_recv.at[1], (h + k) % GROUPS, r).start()

    for load in loads[1:]:
        load.wait()

    make_panels(2)
    make_panels(3)
    for d in range(1, GROUPS):
        chosen = sorted_links(links_vec, (h + d) % GROUPS, h)
        for i in range(CAP):
            place = (chosen[i] - h * OWN) * 2
            picked[d - 1, 2 * i] = panels[place]
            picked[d - 1, 2 * i + 1] = panels[place + 1]

    def low_part(k, core):
        return ham_buf.at[(h + GROUPS - k) % GROUPS, core, low]

    def high_part(k, core):
        return ham_buf.at[:, core, high, (y + YS - k) % YS]

    def to_core(part, i):
        remote(part, part, h4_send.at[i], h4_recv.at[i], h, r - c + 1 - c).start()

    wait_bytes(ham_buf.at[h, c, low, pl.ds(0, YS - 1)], h2_recv.at[0])
    for k in (1, 3, 2):
        part = low_part(0, c)
        remote(part, part, h3_send.at[k - 1], h3_recv.at[k - 1], (h + k) % GROUPS, r).start()
    wait_bytes(ham_buf.at[pl.ds(0, GROUPS - 1), c, high, y], h2_recv.at[1])
    for k in (1, 3, 2):
        part = high_part(0, c)
        remote(part, part, h3_send.at[k + 2], h3_recv.at[k + 2], h, y_row(k)).start()
    to_core(low_part(0, c), 0)
    to_core(high_part(0, c), GROUPS)

    def forward_in(j):
        wait_bytes(z_in.at[j], zi_recv.at[j])

        def send_y(k):
            there, row = other_yc(k)
            remote(
                z_in.at[j, :, there // 2, :, pl.ds(pl.multiple_of(there % 2 * HALF, HALF), HALF)],
                y_in.at[j, :, yc], yi_send.at[j], yi_recv.at[j], h, row,
            ).start()

        pltpu.make_async_copy(
            z_in.at[j, :, y, :, pl.ds(pl.multiple_of(c * HALF, HALF), HALF)], y_in.at[j, :, yc], yi_recv.at[j]
        ).start()
        each(1, YC, send_y)

    def take(q, k):
        cols = pl.ds(pl.multiple_of(q * QUART, QUART), QUART)
        for cc in range(2):
            hi, lo = split(ham_buf[q, cc, k // YS, k % YS])
            rows = pl.ds(pl.multiple_of((k * 2 + cc) * ROWS, ROWS), ROWS)
            ham_hi[rows, cols] = hi
            ham_lo[rows, cols] = lo

    def take_low(k):
        wait_bytes(low_part(k, 1 - c), h4_recv.at[k])
        q = (h + GROUPS - k) % GROUPS
        each(0, ZS * YS // 2, lambda i: take(q, i))

    def take_high(k):
        wait_bytes(high_part(k, 1 - c), h4_recv.at[GROUPS + k])
        yy = (y + YS - k) % YS
        each(0, ZS // 2 * GROUPS, lambda i: take(i // (ZS // 2), (ZS // 2 + i % (ZS // 2)) * YS + yy))

    def multiply_left(j):
        wait_bytes(y_in.at[j], yi_recv.at[j])

        def cut(k):
            hi, lo = split(y_in[j, k].reshape(YC * ROWS, HALF))
            rows = pl.ds(pl.multiple_of(k * YC * ROWS, YC * ROWS), YC * ROWS)
            right_cat[rows, 0:HALF] = hi
            right_cat[rows, HALF:WIDE] = lo

        each(0, ZS, cut)

        def tile(k):
            rows = pl.ds(pl.multiple_of(k * TILE, TILE), TILE)
            both = dot(ham_hi[rows, :], right_cat[...])
            value = both[:, HALF:] + dot(ham_lo[rows, :], right_cat[:, 0:HALF]) + both[:, :HALF]
            left[j, pl.ds(k * 2, 2)] = value.reshape(2, YC, ROWS, HALF)

        each(0, N // TILE, tile)

        def send_y(k):
            there, row = other_yc(k)
            remote(
                left.at[j, :, there], y_back.at[j, :, y, :, pl.ds(pl.multiple_of(c * HALF, HALF), HALF)],
                yb_send.at[j], yb_recv.at[j], h, row,
            ).start()

        pltpu.make_async_copy(
            left.at[j, :, yc], y_back.at[j, :, y, :, pl.ds(pl.multiple_of(c * HALF, HALF), HALF)], yb_recv.at[j]
        ).start()
        each(1, YC, send_y)

    def forward_back(j):
        wait_bytes(y_back.at[j], yb_recv.at[j])

        def send_z(k):
            there, row = other_z(k)
            remote(
                y_back.at[j, there], z_back.at[j, pl.ds(z * YS, YS)], zb_send.at[j], zb_recv.at[j], h, row
            ).start()

        pltpu.make_async_copy(y_back.at[j, z], z_back.at[j, pl.ds(z * YS, YS)], zb_recv.at[j]).start()
        each(1, ZS, send_z)

    def multiply_right(k):
        rows = pl.ds(k * (TILE // ROWS), TILE // ROWS)
        hi, lo = split(panels[rows].reshape(TILE, N))

        def columns(q):
            cols = pl.ds(pl.multiple_of(q * TILE, TILE), TILE)
            top = ham_hi[:, cols]
            value = dot(hi, ham_lo[:, cols]) + dot(lo, top) + dot(hi, top)
            value = value.reshape(TILE // ROWS // 2, 2, ROWS, TILE)
            pairs = pl.ds(k * (TILE // ROWS // 2), TILE // ROWS // 2)
            acc[pairs, 0, :, cols] = acc[pairs, 0, :, cols] - value[:, 1]
            acc[pairs, 1, :, cols] = acc[pairs, 1, :, cols] + value[:, 0]

        each(0, N // TILE, columns)

    def decay(a):
        rate = damping[a]
        first, second = panels[2 * a], panels[2 * a + 1]
        acc[a, 0] = -(rate * first)
        acc[a, 1] = -(rate * second)
        pool[2 * a] = first
        pool[2 * a + 1] = second

    each(0, OWN, decay)

    lane = lax.broadcasted_iota(jnp.int32, (ROWS, N), 1)
    diagonal = lane == lax.broadcasted_iota(jnp.int32, (ROWS, N), 0) + r * ROWS
    for k in range(BATH):
        columns = jnp.broadcast_to(modes[k : k + 1, :], (ROWS, N))
        row_part = jnp.sum(jnp.where(diagonal, columns, 0.0), axis=1, keepdims=True)
        gap[k] = row_part - columns
        total[k] = row_part + columns

    sent_chunk(0)
    start_chunk(2)
    forward_in(0)
    sent_chunk(1)
    start_chunk(3)
    forward_in(1)
    take_low(0)
    take_high(0)
    for k in (1, 3, 2):
        wait_bytes(low_part(k, c), h3_recv.at[k - 1])
        to_core(low_part(k, c), k)
        wait_bytes(high_part(k, c), h3_recv.at[k + 2])
        to_core(high_part(k, c), GROUPS + k)
    for k in (1, 2, 3):
        remote(
            picked.at[k - 1], pool.at[pl.ds(MATS + (k - 1) * 2 * CAP, 2 * CAP)],
            pick_send.at[k - 1], pick_recv.at[k - 1], (h + k) % GROUPS, r,
        ).start()
    for k in (1, 3, 2):
        take_low(k)
        take_high(k)
    multiply_left(0)
    multiply_left(1)
    forward_in(2)
    forward_back(0)
    forward_in(3)
    forward_back(1)
    multiply_left(2)
    forward_back(2)
    multiply_left(3)
    forward_back(3)
    each(0, MATS * ROWS // TILE, multiply_right)

    for d in range(1, GROUPS):
        wait_bytes(pool.at[pl.ds(MATS + (d - 1) * 2 * CAP, 2 * CAP)], pick_recv.at[d - 1])
    names = []
    for d in range(1, GROUPS):
        names += sorted_links(links_vec, h, (h + GROUPS - d) % GROUPS)

    def couple(a):
        real, imag = acc[a, 0], acc[a, 1]
        for slot in range(SLOTS):
            link = links[slot, h * OWN + a]
            mode = bath[slot, h * OWN + a]
            kind = kinds[slot, h * OWN + a]
            place = link - h * OWN
            for i, name in enumerate(names):
                place = jnp.where(link == name, OWN + i, place)
            direct = jnp.where(kind == 1, 1.0, jnp.where(kind == 2, coeff[0, mode], 0.0))
            mixing = jnp.where(kind == 2, coeff[1, mode], 0.0)
            first, second = pool[2 * place], pool[2 * place + 1]
            across = direct * gap[mode]
            along = mixing * total[mode]
            real = real + (across * second + along * first)
            imag = imag + (along * second - across * first)
        acc[a, 0], acc[a, 1] = real, imag

    each(0, OWN, couple)

    for j in range(CHUNKS):
        cols = pl.ds(j * WIDE, WIDE)
        wait_bytes(z_back.at[j], zb_recv.at[j])

        def finish(k, j=j, cols=cols):
            part = pl.ds(k * 2, 2)
            back = z_back[j, pl.ds(k * 4, 4)].reshape(2, 2, ROWS, WIDE)
            real = acc[part, 0, :, cols] + back[:, 1]
            imag = acc[part, 1, :, cols] - back[:, 0]
            acc[part, 0, :, cols] = real
            acc[part, 1, :, cols] = imag
            new[part, 0, :, cols] = new[part, 0, :, cols] + third_step * real
            new[part, 1, :, cols] = new[part, 1, :, cols] + third_step * imag

        each(0, OWN // 2, finish)

    wait_bytes(ham_buf.at[0, 0, pl.ds(0, ZS - 1), 0], h1_send)
    wait_bytes(ham_buf.at[0, 0, low, pl.ds(0, YS - 1)], h2_send.at[0])
    wait_bytes(ham_buf.at[0, 0, high, pl.ds(0, YS - 1)], h2_send.at[1])
    for k in range(2 * GROUPS - 2):
        wait_bytes(ham_buf.at[0, 0, low], h3_send.at[k])
    for k in range(2 * GROUPS):
        wait_bytes(ham_buf.at[0, 0, low], h4_send.at[k])
    for k in range(GROUPS - 1):
        wait_bytes(picked.at[0], pick_send.at[k])
    for j in range(CHUNKS):
        if j >= 2:
            sent_chunk(j)
        wait_bytes(y_in.at[0, :, pl.ds(0, YC - 1)], yi_send.at[j])
        wait_bytes(left.at[0, :, pl.ds(0, YC - 1)], yb_send.at[j])
        wait_bytes(y_back.at[0, pl.ds(0, ZS - 1)], zb_send.at[j])


def section(*arrays):
    f32, bf16, i32 = jnp.float32, jnp.bfloat16, jnp.int32
    dma = pltpu.SemaphoreType.DMA
    four = (CHUNKS,)
    outs = [pltpu.VMEM((OWN, 2, ROWS, N), f32)] * 2
    return pl.pallas_call(
        kernel,
        out_shape=outs,
        in_specs=[pl.BlockSpec(memory_space=pltpu.HBM)] * len(arrays),
        out_specs=[pl.BlockSpec(memory_space=pltpu.VMEM)] * 2,
        scratch_shapes=[
            pltpu.VMEM((ROWS, N), f32),
            pltpu.VMEM((BATH, N), f32),
            pltpu.SMEM((2, BATH), f32),
            pltpu.SMEM((OWN,), f32),
            pltpu.VMEM((SLOTS, GROUPS * OWN), i32),
            pltpu.SMEM((SLOTS, GROUPS * OWN), i32),
            pltpu.SMEM((SLOTS, GROUPS * OWN), i32),
            pltpu.SMEM((SLOTS, GROUPS * OWN), i32),
            pltpu.VMEM((MATS, ROWS, N), f32),
            pltpu.VMEM((MATS, ROWS, N), f32),
            pltpu.VMEM((MATS, ROWS, N), f32),
            pltpu.VMEM((GROUPS, 2, ZS, YS, ROWS, QUART), f32),
            pltpu.VMEM((N, N), bf16),
            pltpu.VMEM((N, N), bf16),
            pltpu.VMEM((CHUNKS, ZS, YS, ROWS, WIDE), f32),
            pltpu.VMEM((CHUNKS, ZS, YC, ROWS, HALF), f32),
            pltpu.VMEM((N, WIDE), bf16),
            pltpu.VMEM((CHUNKS, ZS, YC, ROWS, HALF), f32),
            pltpu.VMEM((CHUNKS, ZS, YS, ROWS, WIDE), f32),
            pltpu.VMEM((CHUNKS, MATS, ROWS, WIDE), f32),
            pltpu.VMEM((MATS + (GROUPS - 1) * 2 * CAP, ROWS, N), f32),
            pltpu.VMEM((GROUPS - 1, 2 * CAP, ROWS, N), f32),
            pltpu.VMEM((BATH, ROWS, N), f32),
            pltpu.VMEM((BATH, ROWS, N), f32),
            dma(four), dma(four), dma((9,)),
            dma, dma, dma((2,)), dma((2,)),
            dma((6,)), dma((6,)), dma((8,)), dma((8,)),
            dma(four), dma(four), dma(four), dma(four),
            dma(four), dma(four), dma(four), dma(four),
            dma((3,)), dma((3,)),
        ],
        compiler_params=pltpu.CompilerParams(
            collective_id=0, has_side_effects=True, vmem_limit_bytes=48 * 1024 * 1024
        ),
        cost_estimate=pl.CostEstimate(flops=6 * 2**30, bytes_accessed=6 * 2**20, transcendentals=0),
        name="section",
    )(*[pltpu.with_memory_space_constraint(array, pltpu.HBM) for array in arrays])


def store_kernel(deriv, new, deriv_out, new_out, sem):
    copies = [
        pltpu.make_async_copy(deriv, deriv_out, sem.at[0]),
        pltpu.make_async_copy(new, new_out, sem.at[1]),
    ]
    for copy in copies:
        copy.start()
    for copy in copies:
        copy.wait()


def store(deriv, new):
    shape = jax.ShapeDtypeStruct(deriv.shape, deriv.dtype)
    return pl.pallas_call(
        store_kernel,
        out_shape=[shape] * 2,
        in_specs=[pl.BlockSpec(memory_space=pltpu.VMEM)] * 2,
        out_specs=[pl.BlockSpec(memory_space=pltpu.HBM)] * 2,
        scratch_shapes=[pltpu.SemaphoreType.DMA((2,))],
        compiler_params=pltpu.CompilerParams(vmem_limit_bytes=8 * 1024 * 1024),
        cost_estimate=pl.CostEstimate(flops=0, bytes_accessed=4 * 2**20, transcendentals=0),
        name="store",
    )(*[pltpu.with_memory_space_constraint(array, pltpu.VMEM) for array in (deriv, new)])


def local(rho, incr, accum, ham, modes, coeff, damping, links, bath, kinds):
    deriv, new = section(
        rho.reshape(MATS, ROWS, N), incr.reshape(MATS, ROWS, N), accum, ham, modes, coeff, damping,
        links.T, bath.T, kinds.T,
    )
    return store(deriv, new)


def solution(mesh):
    in_specs = (
        P("hier", None, "row", None),
        P("hier", None, "row", None),
        P("hier", None, "row", None),
        P("row", None),
        P(),
        P(),
        P("hier"),
        P(),
        P(),
        P(),
    )
    out_specs = (P("hier", None, "row", None), P("hier", None, "row", None))
    return jax.shard_map(local, mesh=mesh, in_specs=in_specs, out_specs=out_specs, check_vma=False)
```

```python
import jax
import jax.numpy as jnp
from jax import lax
from jax.experimental import pallas as pl
from jax.experimental.pallas import tpu as pltpu
from jax.sharding import PartitionSpec as P

half_step = 0.1
third_step = 0.2 / 3.0

MESH = pl.DeviceIdType.MESH
GROUPS = 4
ZS = 8
YS = 4
YC = 8
OWN = 16
CAP = 4
MATS = 32
ROWS = 16
N = 1024
BATH = 8
SLOTS = 4
CHUNKS = 4
WIDE = N // CHUNKS
HALF = WIDE // 2
QUART = N // GROUPS
TILE = 256
PIECES = 4


def split(x):
    hi = x.astype(jnp.bfloat16)
    return hi, (x - hi.astype(jnp.float32)).astype(jnp.bfloat16)


def dot(a, b):
    return jnp.dot(a, b, preferred_element_type=jnp.float32)


def sorted_links(links_vec, rows_of, target):
    block = links_vec[...]
    member = lax.broadcasted_iota(jnp.int32, block.shape, 1) - rows_of * OWN
    mine = (member >= 0) & (member < OWN)
    low = target * OWN
    found, last = [], low - 1
    for _ in range(CAP):
        inside = mine & (block > last) & (block < low + OWN)
        last = jnp.minimum(jnp.min(jnp.where(inside, block, low + OWN - 1)), low + OWN - 1)
        found.append(last)
    return found


def kernel(
    rho, incr, accum, ham_hbm, modes_hbm, coeff_hbm, damping_hbm, links_hbm, bath_hbm, kinds_hbm,
    acc, new,
    ham, modes, coeff, damping, links_vec, links, bath, kinds,
    panels, rho_buf, incr_buf, ham_buf, ham_hi, ham_lo, z_in, y_in, right_cat, left, y_back, z_back,
    pool, picked, gap, total,
    rho_sem, incr_sem, load_sem, h1_send, h1_recv, h2_send, h2_recv, h3_send, h3_recv, h4_send, h4_recv,
    zi_send, zi_recv, yi_send, yi_recv, yb_send, yb_recv, zb_send, zb_recv, pick_send, pick_recv,
):
    h = lax.axis_index("hier")
    r = lax.axis_index("row")
    z = r // YC
    yc = r % YC
    y = yc // 2
    c = yc % 2

    def remote(src, dst, send, recv, group, row):
        return pltpu.make_async_remote_copy(
            src_ref=src, dst_ref=dst, send_sem=send, recv_sem=recv,
            device_id=(group, row), device_id_type=MESH,
        )

    def wait_bytes(ref, sem):
        pltpu.make_async_copy(ref, ref, sem).wait()

    def other_z(k):
        there = (z + ZS // 2 + k // 2 * (2 * (k % 2) - 1) + ZS) % ZS
        return there, there * YC + yc

    def other_yc(k):
        there = (yc + k) % YC
        return there, z * YC + there

    def each(first, last, body):
        def step(k, carry):
            body(k)
            return carry

        lax.fori_loop(first, last, step, 0)

    def load_panel(j):
        part = (slice(None), slice(None), pl.ds(j * WIDE, WIDE))
        return (
            pltpu.make_async_copy(rho.at[part], rho_buf.at[part], rho_sem.at[j]),
            pltpu.make_async_copy(incr.at[part], incr_buf.at[part], incr_sem.at[j]),
        )

    pairs = [
        (ham_hbm, ham), (modes_hbm, modes), (coeff_hbm, coeff), (damping_hbm, damping), (links_hbm, links_vec),
        (links_hbm, links), (bath_hbm, bath), (kinds_hbm, kinds), (accum, new),
    ]
    loads = [pltpu.make_async_copy(src, dst, load_sem.at[i]) for i, (src, dst) in enumerate(pairs)]
    loads[0].start()
    for load in load_panel(0):
        load.start()
    barrier = pltpu.get_barrier_semaphore()

    def greet(group, row):
        pl.semaphore_signal(barrier, inc=1, device_id=(group, row), device_id_type=MESH)

    each(1, ZS, lambda k: greet(h, other_z(k)[1]))
    each(1, YC, lambda k: greet(h, other_yc(k)[1]))
    each(1, GROUPS, lambda k: greet((h + k) % GROUPS, r))

    def make_panels(j):
        for load in load_panel(j):
            load.wait()
        cols = pl.ds(j * WIDE, WIDE)

        def make(m):
            part = pl.ds(m * 8, 8)
            panels[part, :, cols] = rho_buf[part, :, cols] + half_step * incr_buf[part, :, cols]

        each(0, MATS // 8, make)

    loads[0].wait()
    pl.semaphore_wait(barrier, ZS - 1 + YC - 1 + GROUPS - 1)

    ham_own = ham.at[:, pl.ds(pl.multiple_of(h * QUART, QUART), QUART)]
    h1_local = pltpu.make_async_copy(ham_own, ham_buf.at[h, c, z, y], h1_recv)
    h1_local.start()
    each(1, ZS, lambda k: remote(ham_own, ham_buf.at[h, c, z, y], h1_send, h1_recv, h, other_z(k)[1]).start())

    def start_chunk(j):
        if j < 2:
            make_panels(j)
        cols = pl.ds(j * WIDE, WIDE)

        def send_z(k):
            there, row = other_z(k)
            remote(
                panels.at[pl.ds(there * YS, YS), :, cols], z_in.at[j, z], zi_send.at[j], zi_recv.at[j], h, row
            ).start()

        pltpu.make_async_copy(panels.at[pl.ds(z * YS, YS), :, cols], z_in.at[j, z], zi_recv.at[j]).start()
        each(1, ZS, send_z)

    def sent_chunk(j):
        wait_bytes(z_in.at[0, pl.ds(0, ZS - 1)], zi_send.at[j])

    start_chunk(0)
    for j in range(1, CHUNKS):
        for load in load_panel(j):
            load.start()
    for load in loads[1:]:
        load.start()
    start_chunk(1)

    wait_bytes(ham_buf.at[h, c, :, y], h1_recv)
    low, high = pl.ds(0, ZS // 2), pl.ds(ZS // 2, ZS // 2)

    def y_row(k):
        return z * YC + (y + k) % YS * 2 + c

    for k in (1, 3, 2):
        part = ham_buf.at[h, c, low, y]
        remote(part, part, h2_send.at[0], h2_recv.at[0], h, y_row(k)).start()
        part = ham_buf.at[h, c, high, y]
        remote(part, part, h2_send.at[1], h2_recv.at[1], (h + k) % GROUPS, r).start()

    for load in loads[1:]:
        load.wait()

    make_panels(2)
    make_panels(3)
    for d in range(1, GROUPS):
        chosen = sorted_links(links_vec, (h + d) % GROUPS, h)
        for i in range(CAP):
            place = (chosen[i] - h * OWN) * 2
            picked[d - 1, 2 * i] = panels[place]
            picked[d - 1, 2 * i + 1] = panels[place + 1]

    def low_part(k, core):
        return ham_buf.at[(h + GROUPS - k) % GROUPS, core, low]

    def high_part(k, core):
        return ham_buf.at[:, core, high, (y + YS - k) % YS]

    def to_core(part, i):
        remote(part, part, h4_send.at[i], h4_recv.at[i], h, r - c + 1 - c).start()

    wait_bytes(ham_buf.at[h, c, low, pl.ds(0, YS - 1)], h2_recv.at[0])
    for k in (1, 3, 2):
        part = low_part(0, c)
        remote(part, part, h3_send.at[k - 1], h3_recv.at[k - 1], (h + k) % GROUPS, r).start()
    wait_bytes(ham_buf.at[pl.ds(0, GROUPS - 1), c, high, y], h2_recv.at[1])
    for k in (1, 3, 2):
        part = high_part(0, c)
        remote(part, part, h3_send.at[k + 2], h3_recv.at[k + 2], h, y_row(k)).start()
    to_core(low_part(0, c), 0)
    to_core(high_part(0, c), GROUPS)

    def forward_in(j):
        wait_bytes(z_in.at[j], zi_recv.at[j])

        def send_y(k):
            there, row = other_yc(k)
            remote(
                z_in.at[j, :, there // 2, :, pl.ds(pl.multiple_of(there % 2 * HALF, HALF), HALF)],
                y_in.at[j, :, yc], yi_send.at[j], yi_recv.at[j], h, row,
            ).start()

        pltpu.make_async_copy(
            z_in.at[j, :, y, :, pl.ds(pl.multiple_of(c * HALF, HALF), HALF)], y_in.at[j, :, yc], yi_recv.at[j]
        ).start()
        each(1, YC, send_y)

    def take(q, k):
        cols = pl.ds(pl.multiple_of(q * QUART, QUART), QUART)
        for cc in range(2):
            hi, lo = split(ham_buf[q, cc, k // YS, k % YS])
            rows = pl.ds(pl.multiple_of((k * 2 + cc) * ROWS, ROWS), ROWS)
            ham_hi[rows, cols] = hi
            ham_lo[rows, cols] = lo

    def take_low(k):
        wait_bytes(low_part(k, 1 - c), h4_recv.at[k])
        q = (h + GROUPS - k) % GROUPS
        each(0, ZS * YS // 2, lambda i: take(q, i))

    def take_high(k):
        wait_bytes(high_part(k, 1 - c), h4_recv.at[GROUPS + k])
        yy = (y + YS - k) % YS
        each(0, ZS // 2 * GROUPS, lambda i: take(i // (ZS // 2), (ZS // 2 + i % (ZS // 2)) * YS + yy))

    def multiply_left(j):
        wait_bytes(y_in.at[j], yi_recv.at[j])

        def cut(k):
            hi, lo = split(y_in[j, k].reshape(YC * ROWS, HALF))
            rows = pl.ds(pl.multiple_of(k * YC * ROWS, YC * ROWS), YC * ROWS)
            right_cat[rows, 0:HALF] = hi
            right_cat[rows, HALF:WIDE] = lo

        each(0, ZS, cut)

        def tile(k):
            rows = pl.ds(pl.multiple_of(k * TILE, TILE), TILE)
            both = dot(ham_hi[rows, :], right_cat[...])
            value = both[:, HALF:] + dot(ham_lo[rows, :], right_cat[:, 0:HALF]) + both[:, :HALF]
            left[j, pl.ds(k * 2, 2)] = value.reshape(2, YC, ROWS, HALF)

        each(0, N // TILE, tile)

        def send_y(k):
            there, row = other_yc(k)
            remote(
                left.at[j, :, there], y_back.at[j, :, y, :, pl.ds(pl.multiple_of(c * HALF, HALF), HALF)],
                yb_send.at[j], yb_recv.at[j], h, row,
            ).start()

        pltpu.make_async_copy(
            left.at[j, :, yc], y_back.at[j, :, y, :, pl.ds(pl.multiple_of(c * HALF, HALF), HALF)], yb_recv.at[j]
        ).start()
        each(1, YC, send_y)

    def forward_back(j):
        wait_bytes(y_back.at[j], yb_recv.at[j])

        def send_z(k):
            there, row = other_z(k)
            remote(
                y_back.at[j, there], z_back.at[j, pl.ds(z * YS, YS)], zb_send.at[j], zb_recv.at[j], h, row
            ).start()

        pltpu.make_async_copy(y_back.at[j, z], z_back.at[j, pl.ds(z * YS, YS)], zb_recv.at[j]).start()
        each(1, ZS, send_z)

    def multiply_right(k):
        rows = pl.ds(k * (TILE // ROWS), TILE // ROWS)
        hi, lo = split(panels[rows].reshape(TILE, N))

        def columns(q):
            cols = pl.ds(pl.multiple_of(q * TILE, TILE), TILE)
            top = ham_hi[:, cols]
            value = dot(hi, ham_lo[:, cols]) + dot(lo, top) + dot(hi, top)
            value = value.reshape(TILE // ROWS // 2, 2, ROWS, TILE)
            pairs = pl.ds(k * (TILE // ROWS // 2), TILE // ROWS // 2)
            acc[pairs, 0, :, cols] = acc[pairs, 0, :, cols] - value[:, 1]
            acc[pairs, 1, :, cols] = acc[pairs, 1, :, cols] + value[:, 0]

        each(0, N // TILE, columns)

    def decay(a):
        rate = damping[a]
        first, second = panels[2 * a], panels[2 * a + 1]
        acc[a, 0] = -(rate * first)
        acc[a, 1] = -(rate * second)
        pool[2 * a] = first
        pool[2 * a + 1] = second

    each(0, OWN, decay)

    lane = lax.broadcasted_iota(jnp.int32, (ROWS, N), 1)
    diagonal = lane == lax.broadcasted_iota(jnp.int32, (ROWS, N), 0) + r * ROWS
    for k in range(BATH):
        columns = jnp.broadcast_to(modes[k : k + 1, :], (ROWS, N))
        row_part = jnp.sum(jnp.where(diagonal, columns, 0.0), axis=1, keepdims=True)
        gap[k] = row_part - columns
        total[k] = row_part + columns

    sent_chunk(0)
    start_chunk(2)
    forward_in(0)
    sent_chunk(1)
    start_chunk(3)
    forward_in(1)
    take_low(0)
    take_high(0)
    for k in (1, 3, 2):
        wait_bytes(low_part(k, c), h3_recv.at[k - 1])
        to_core(low_part(k, c), k)
        wait_bytes(high_part(k, c), h3_recv.at[k + 2])
        to_core(high_part(k, c), GROUPS + k)
    for k in (1, 2, 3):
        remote(
            picked.at[k - 1], pool.at[pl.ds(MATS + (k - 1) * 2 * CAP, 2 * CAP)],
            pick_send.at[k - 1], pick_recv.at[k - 1], (h + k) % GROUPS, r,
        ).start()
    for k in (1, 3, 2):
        take_low(k)
        take_high(k)
    multiply_left(0)
    multiply_left(1)
    forward_in(2)
    forward_back(0)
    forward_in(3)
    forward_back(1)
    multiply_left(2)
    forward_back(2)
    multiply_left(3)
    forward_back(3)
    each(0, MATS * ROWS // TILE, multiply_right)

    for d in range(1, GROUPS):
        wait_bytes(pool.at[pl.ds(MATS + (d - 1) * 2 * CAP, 2 * CAP)], pick_recv.at[d - 1])
    names = []
    for d in range(1, GROUPS):
        names += sorted_links(links_vec, h, (h + GROUPS - d) % GROUPS)

    def couple(a):
        real, imag = acc[a, 0], acc[a, 1]
        for slot in range(SLOTS):
            link = links[slot, h * OWN + a]
            mode = bath[slot, h * OWN + a]
            kind = kinds[slot, h * OWN + a]
            place = link - h * OWN
            for i, name in enumerate(names):
                place = jnp.where(link == name, OWN + i, place)
            direct = jnp.where(kind == 1, 1.0, jnp.where(kind == 2, coeff[0, mode], 0.0))
            mixing = jnp.where(kind == 2, coeff[1, mode], 0.0)
            first, second = pool[2 * place], pool[2 * place + 1]
            across = direct * gap[mode]
            along = mixing * total[mode]
            real = real + (across * second + along * first)
            imag = imag + (along * second - across * first)
        acc[a, 0], acc[a, 1] = real, imag

    each(0, OWN, couple)

    for j in range(CHUNKS):
        cols = pl.ds(j * WIDE, WIDE)
        wait_bytes(z_back.at[j], zb_recv.at[j])

        def finish(k, j=j, cols=cols):
            part = pl.ds(k * 2, 2)
            back = z_back[j, pl.ds(k * 4, 4)].reshape(2, 2, ROWS, WIDE)
            real = acc[part, 0, :, cols] + back[:, 1]
            imag = acc[part, 1, :, cols] - back[:, 0]
            acc[part, 0, :, cols] = real
            acc[part, 1, :, cols] = imag
            new[part, 0, :, cols] = new[part, 0, :, cols] + third_step * real
            new[part, 1, :, cols] = new[part, 1, :, cols] + third_step * imag

        each(0, OWN // 2, finish)

    wait_bytes(ham_buf.at[0, 0, pl.ds(0, ZS - 1), 0], h1_send)
    wait_bytes(ham_buf.at[0, 0, low, pl.ds(0, YS - 1)], h2_send.at[0])
    wait_bytes(ham_buf.at[0, 0, high, pl.ds(0, YS - 1)], h2_send.at[1])
    for k in range(2 * GROUPS - 2):
        wait_bytes(ham_buf.at[0, 0, low], h3_send.at[k])
    for k in range(2 * GROUPS):
        wait_bytes(ham_buf.at[0, 0, low], h4_send.at[k])
    for k in range(GROUPS - 1):
        wait_bytes(picked.at[0], pick_send.at[k])
    for j in range(CHUNKS):
        if j >= 2:
            sent_chunk(j)
        wait_bytes(y_in.at[0, :, pl.ds(0, YC - 1)], yi_send.at[j])
        wait_bytes(left.at[0, :, pl.ds(0, YC - 1)], yb_send.at[j])
        wait_bytes(y_back.at[0, pl.ds(0, ZS - 1)], zb_send.at[j])


def section(*arrays):
    f32, bf16, i32 = jnp.float32, jnp.bfloat16, jnp.int32
    dma = pltpu.SemaphoreType.DMA
    four = (CHUNKS,)
    outs = [pltpu.VMEM((OWN, 2, ROWS, N), f32)] * 2
    return pl.pallas_call(
        kernel,
        out_shape=outs,
        in_specs=[pl.BlockSpec(memory_space=pltpu.HBM)] * len(arrays),
        out_specs=[pl.BlockSpec(memory_space=pltpu.VMEM)] * 2,
        scratch_shapes=[
            pltpu.VMEM((ROWS, N), f32),
            pltpu.VMEM((BATH, N), f32),
            pltpu.SMEM((2, BATH), f32),
            pltpu.SMEM((OWN,), f32),
            pltpu.VMEM((SLOTS, GROUPS * OWN), i32),
            pltpu.SMEM((SLOTS, GROUPS * OWN), i32),
            pltpu.SMEM((SLOTS, GROUPS * OWN), i32),
            pltpu.SMEM((SLOTS, GROUPS * OWN), i32),
            pltpu.VMEM((MATS, ROWS, N), f32),
            pltpu.VMEM((MATS, ROWS, N), f32),
            pltpu.VMEM((MATS, ROWS, N), f32),
            pltpu.VMEM((GROUPS, 2, ZS, YS, ROWS, QUART), f32),
            pltpu.VMEM((N, N), bf16),
            pltpu.VMEM((N, N), bf16),
            pltpu.VMEM((CHUNKS, ZS, YS, ROWS, WIDE), f32),
            pltpu.VMEM((CHUNKS, ZS, YC, ROWS, HALF), f32),
            pltpu.VMEM((N, WIDE), bf16),
            pltpu.VMEM((CHUNKS, ZS, YC, ROWS, HALF), f32),
            pltpu.VMEM((CHUNKS, ZS, YS, ROWS, WIDE), f32),
            pltpu.VMEM((CHUNKS, MATS, ROWS, WIDE), f32),
            pltpu.VMEM((MATS + (GROUPS - 1) * 2 * CAP, ROWS, N), f32),
            pltpu.VMEM((GROUPS - 1, 2 * CAP, ROWS, N), f32),
            pltpu.VMEM((BATH, ROWS, N), f32),
            pltpu.VMEM((BATH, ROWS, N), f32),
            dma(four), dma(four), dma((9,)),
            dma, dma, dma((2,)), dma((2,)),
            dma((6,)), dma((6,)), dma((8,)), dma((8,)),
            dma(four), dma(four), dma(four), dma(four),
            dma(four), dma(four), dma(four), dma(four),
            dma((3,)), dma((3,)),
        ],
        compiler_params=pltpu.CompilerParams(
            collective_id=0, has_side_effects=True, vmem_limit_bytes=48 * 1024 * 1024
        ),
        cost_estimate=pl.CostEstimate(flops=6 * 2**30, bytes_accessed=6 * 2**20, transcendentals=0),
        name="section",
    )(*[pltpu.with_memory_space_constraint(array, pltpu.HBM) for array in arrays])


def store_kernel(deriv, new, deriv_out, new_out, sem):
    copies = []
    for i in range(PIECES):
        part = pl.ds(i * (OWN // PIECES), OWN // PIECES)
        copies.append(pltpu.make_async_copy(deriv.at[part], deriv_out.at[part], sem.at[0, i]))
        copies.append(pltpu.make_async_copy(new.at[part], new_out.at[part], sem.at[1, i]))
    for copy in copies:
        copy.start()
    for copy in copies:
        copy.wait()


def store(deriv, new):
    shape = jax.ShapeDtypeStruct(deriv.shape, deriv.dtype)
    return pl.pallas_call(
        store_kernel,
        out_shape=[shape] * 2,
        in_specs=[pl.BlockSpec(memory_space=pltpu.VMEM)] * 2,
        out_specs=[pl.BlockSpec(memory_space=pltpu.HBM)] * 2,
        scratch_shapes=[pltpu.SemaphoreType.DMA((2, PIECES))],
        compiler_params=pltpu.CompilerParams(vmem_limit_bytes=8 * 1024 * 1024),
        cost_estimate=pl.CostEstimate(flops=0, bytes_accessed=4 * 2**20, transcendentals=0),
        name="store",
    )(*[pltpu.with_memory_space_constraint(array, pltpu.VMEM) for array in (deriv, new)])


def local(rho, incr, accum, ham, modes, coeff, damping, links, bath, kinds):
    deriv, new = section(
        rho.reshape(MATS, ROWS, N), incr.reshape(MATS, ROWS, N), accum, ham, modes, coeff, damping,
        links.T, bath.T, kinds.T,
    )
    return store(deriv, new)


def solution(mesh):
    in_specs = (
        P("hier", None, "row", None),
        P("hier", None, "row", None),
        P("hier", None, "row", None),
        P("row", None),
        P(),
        P(),
        P("hier"),
        P(),
        P(),
        P(),
    )
    out_specs = (P("hier", None, "row", None), P("hier", None, "row", None))
    return jax.shard_map(local, mesh=mesh, in_specs=in_specs, out_specs=out_specs, check_vma=False)
```

```python
import jax
import jax.numpy as jnp
from jax import lax
from jax.experimental import pallas as pl
from jax.experimental.pallas import tpu as pltpu
from jax.sharding import PartitionSpec as P

half_step = 0.1
third_step = 0.2 / 3.0

MESH = pl.DeviceIdType.MESH
GROUPS = 4
ZS = 8
YS = 4
YC = 8
OWN = 16
CAP = 4
MATS = 32
ROWS = 16
N = 1024
BATH = 8
SLOTS = 4
CHUNKS = 4
WIDE = N // CHUNKS
HALF = WIDE // 2
QUART = N // GROUPS
TILE = 256
PIECES = 4


def split(x):
    hi = x.astype(jnp.bfloat16)
    return hi, (x - hi.astype(jnp.float32)).astype(jnp.bfloat16)


def dot(a, b):
    return jnp.dot(a, b, preferred_element_type=jnp.float32)


def sorted_links(links_vec, rows_of, target):
    block = links_vec[...]
    member = lax.broadcasted_iota(jnp.int32, block.shape, 1) - rows_of * OWN
    mine = (member >= 0) & (member < OWN)
    low = target * OWN
    found, last = [], low - 1
    for _ in range(CAP):
        inside = mine & (block > last) & (block < low + OWN)
        last = jnp.minimum(jnp.min(jnp.where(inside, block, low + OWN - 1)), low + OWN - 1)
        found.append(last)
    return found


def kernel(
    rho, incr, accum, ham_hbm, modes_hbm, coeff_hbm, damping_hbm, links_hbm, bath_hbm, kinds_hbm,
    acc, new,
    ham, modes, coeff, damping, links_vec, links, bath, kinds,
    panels, rho_buf, incr_buf, ham_buf, ham_hi, ham_lo, z_in, y_in, right_cat, left, y_back, z_back,
    pool, picked, gap, total,
    line_sem, across_sem, rho_sem, incr_sem, load_sem, h1_send, h1_recv, h2_send, h2_recv, h3_send, h3_recv, h4_send, h4_recv,
    zi_send, zi_recv, yi_send, yi_recv, yb_send, yb_recv, zb_send, zb_recv, pick_send, pick_recv,
):
    h = lax.axis_index("hier")
    r = lax.axis_index("row")
    z = r // YC
    yc = r % YC
    y = yc // 2
    c = yc % 2

    def remote(src, dst, send, recv, group, row):
        return pltpu.make_async_remote_copy(
            src_ref=src, dst_ref=dst, send_sem=send, recv_sem=recv,
            device_id=(group, row), device_id_type=MESH,
        )

    def wait_bytes(ref, sem):
        pltpu.make_async_copy(ref, ref, sem).wait()

    def other_z(k):
        there = (z + ZS // 2 + k // 2 * (2 * (k % 2) - 1) + ZS) % ZS
        return there, there * YC + yc

    def other_yc(k):
        there = (yc + k) % YC
        return there, z * YC + there

    def each(first, last, body):
        def step(k, carry):
            body(k)
            return carry

        lax.fori_loop(first, last, step, 0)

    def load_panel(j):
        part = (slice(None), slice(None), pl.ds(j * WIDE, WIDE))
        return (
            pltpu.make_async_copy(rho.at[part], rho_buf.at[part], rho_sem.at[j]),
            pltpu.make_async_copy(incr.at[part], incr_buf.at[part], incr_sem.at[j]),
        )

    pairs = [
        (ham_hbm, ham), (modes_hbm, modes), (coeff_hbm, coeff), (damping_hbm, damping), (links_hbm, links_vec),
        (links_hbm, links), (bath_hbm, bath), (kinds_hbm, kinds), (accum, new),
    ]
    loads = [pltpu.make_async_copy(src, dst, load_sem.at[i]) for i, (src, dst) in enumerate(pairs)]
    loads[0].start()
    for load in load_panel(0):
        load.start()
    barrier = pltpu.get_barrier_semaphore()

    def greet(group, row):
        pl.semaphore_signal(barrier, inc=1, device_id=(group, row), device_id_type=MESH)

    def across(body):
        each(1, YC, lambda k: body(h, other_yc(k)[1]))
        each(1, GROUPS, lambda k: body((h + k) % GROUPS, r))

    each(1, ZS, lambda k: greet(h, other_z(k)[1]))

    @pl.when(z == 0)
    def _():
        across(greet)


    def make_panels(j):
        for load in load_panel(j):
            load.wait()
        cols = pl.ds(j * WIDE, WIDE)

        def make(m):
            part = pl.ds(m * 8, 8)
            panels[part, :, cols] = rho_buf[part, :, cols] + half_step * incr_buf[part, :, cols]

        each(0, MATS // 8, make)

    loads[0].wait()

    @pl.when(z == 0)
    def _():
        pl.semaphore_wait(barrier, ZS - 1 + YC - 1 + GROUPS - 1)

    @pl.when(z != 0)
    def _():
        pl.semaphore_wait(barrier, ZS - 1)


    ham_own = ham.at[:, pl.ds(pl.multiple_of(h * QUART, QUART), QUART)]
    h1_local = pltpu.make_async_copy(ham_own, ham_buf.at[h, c, z, y], h1_recv)
    h1_local.start()
    each(1, ZS, lambda k: remote(ham_own, ham_buf.at[h, c, z, y], h1_send, h1_recv, h, other_z(k)[1]).start())

    def start_chunk(j):
        if j < 2:
            make_panels(j)
        cols = pl.ds(j * WIDE, WIDE)

        def send_z(k):
            there, row = other_z(k)
            remote(
                panels.at[pl.ds(there * YS, YS), :, cols], z_in.at[j, z], zi_send.at[j], zi_recv.at[j], h, row
            ).start()

        pltpu.make_async_copy(panels.at[pl.ds(z * YS, YS), :, cols], z_in.at[j, z], zi_recv.at[j]).start()
        each(1, ZS, send_z)

    start_chunk(0)

    def signal(sem, group, row):
        pl.semaphore_signal(sem, inc=1, device_id=(group, row), device_id_type=MESH)

    @pl.when(z == 0)
    def _():
        across(lambda group, row: signal(line_sem, group, row))

    for j in range(1, CHUNKS):
        for load in load_panel(j):
            load.start()
    for load in loads[1:]:
        load.start()
    start_chunk(1)
    make_panels(2)
    make_panels(3)
    start_chunk(2)
    start_chunk(3)

    @pl.when(z == 0)
    def _():
        pl.semaphore_wait(line_sem, YC - 1 + GROUPS - 1)
        each(1, ZS, lambda k: signal(across_sem, h, other_z(k)[1]))

    @pl.when(z != 0)
    def _():
        pl.semaphore_wait(across_sem, 1)

    wait_bytes(ham_buf.at[h, c, :, y], h1_recv)
    low, high = pl.ds(0, ZS // 2), pl.ds(ZS // 2, ZS // 2)

    def y_row(k):
        return z * YC + (y + k) % YS * 2 + c

    for k in (1, 3, 2):
        part = ham_buf.at[h, c, low, y]
        remote(part, part, h2_send.at[0], h2_recv.at[0], h, y_row(k)).start()
        part = ham_buf.at[h, c, high, y]
        remote(part, part, h2_send.at[1], h2_recv.at[1], (h + k) % GROUPS, r).start()

    for load in loads[1:]:
        load.wait()

    for d in range(1, GROUPS):
        chosen = sorted_links(links_vec, (h + d) % GROUPS, h)
        for i in range(CAP):
            place = (chosen[i] - h * OWN) * 2
            picked[d - 1, 2 * i] = panels[place]
            picked[d - 1, 2 * i + 1] = panels[place + 1]

    def low_part(k, core):
        return ham_buf.at[(h + GROUPS - k) % GROUPS, core, low]

    def high_part(k, core):
        return ham_buf.at[:, core, high, (y + YS - k) % YS]

    def to_core(part, i):
        remote(part, part, h4_send.at[i], h4_recv.at[i], h, r - c + 1 - c).start()

    wait_bytes(ham_buf.at[h, c, low, pl.ds(0, YS - 1)], h2_recv.at[0])
    for k in (1, 3, 2):
        part = low_part(0, c)
        remote(part, part, h3_send.at[k - 1], h3_recv.at[k - 1], (h + k) % GROUPS, r).start()
    wait_bytes(ham_buf.at[pl.ds(0, GROUPS - 1), c, high, y], h2_recv.at[1])
    for k in (1, 3, 2):
        part = high_part(0, c)
        remote(part, part, h3_send.at[k + 2], h3_recv.at[k + 2], h, y_row(k)).start()
    to_core(low_part(0, c), 0)
    to_core(high_part(0, c), GROUPS)

    def forward_in(j):
        wait_bytes(z_in.at[j], zi_recv.at[j])

        def send_y(k):
            there, row = other_yc(k)
            remote(
                z_in.at[j, :, there // 2, :, pl.ds(pl.multiple_of(there % 2 * HALF, HALF), HALF)],
                y_in.at[j, :, yc], yi_send.at[j], yi_recv.at[j], h, row,
            ).start()

        pltpu.make_async_copy(
            z_in.at[j, :, y, :, pl.ds(pl.multiple_of(c * HALF, HALF), HALF)], y_in.at[j, :, yc], yi_recv.at[j]
        ).start()
        each(1, YC, send_y)

    def take(q, k):
        cols = pl.ds(pl.multiple_of(q * QUART, QUART), QUART)
        for cc in range(2):
            hi, lo = split(ham_buf[q, cc, k // YS, k % YS])
            rows = pl.ds(pl.multiple_of((k * 2 + cc) * ROWS, ROWS), ROWS)
            ham_hi[rows, cols] = hi
            ham_lo[rows, cols] = lo

    def take_low(k):
        wait_bytes(low_part(k, 1 - c), h4_recv.at[k])
        q = (h + GROUPS - k) % GROUPS
        each(0, ZS * YS // 2, lambda i: take(q, i))

    def take_high(k):
        wait_bytes(high_part(k, 1 - c), h4_recv.at[GROUPS + k])
        yy = (y + YS - k) % YS
        each(0, ZS // 2 * GROUPS, lambda i: take(i // (ZS // 2), (ZS // 2 + i % (ZS // 2)) * YS + yy))

    def multiply_left(j):
        wait_bytes(y_in.at[j], yi_recv.at[j])

        def cut(k):
            hi, lo = split(y_in[j, k].reshape(YC * ROWS, HALF))
            rows = pl.ds(pl.multiple_of(k * YC * ROWS, YC * ROWS), YC * ROWS)
            right_cat[rows, 0:HALF] = hi
            right_cat[rows, HALF:WIDE] = lo

        each(0, ZS, cut)

        def tile(k):
            rows = pl.ds(pl.multiple_of(k * TILE, TILE), TILE)
            both = dot(ham_hi[rows, :], right_cat[...])
            value = both[:, HALF:] + dot(ham_lo[rows, :], right_cat[:, 0:HALF]) + both[:, :HALF]
            left[j, pl.ds(k * 2, 2)] = value.reshape(2, YC, ROWS, HALF)

        each(0, N // TILE, tile)

        def send_y(k):
            there, row = other_yc(k)
            remote(
                left.at[j, :, there], y_back.at[j, :, y, :, pl.ds(pl.multiple_of(c * HALF, HALF), HALF)],
                yb_send.at[j], yb_recv.at[j], h, row,
            ).start()

        pltpu.make_async_copy(
            left.at[j, :, yc], y_back.at[j, :, y, :, pl.ds(pl.multiple_of(c * HALF, HALF), HALF)], yb_recv.at[j]
        ).start()
        each(1, YC, send_y)

    def forward_back(j):
        wait_bytes(y_back.at[j], yb_recv.at[j])

        def send_z(k):
            there, row = other_z(k)
            remote(
                y_back.at[j, there], z_back.at[j, pl.ds(z * YS, YS)], zb_send.at[j], zb_recv.at[j], h, row
            ).start()

        pltpu.make_async_copy(y_back.at[j, z], z_back.at[j, pl.ds(z * YS, YS)], zb_recv.at[j]).start()
        each(1, ZS, send_z)

    def multiply_right(k):
        rows = pl.ds(k * (TILE // ROWS), TILE // ROWS)
        hi, lo = split(panels[rows].reshape(TILE, N))

        def columns(q):
            cols = pl.ds(pl.multiple_of(q * TILE, TILE), TILE)
            top = ham_hi[:, cols]
            value = dot(hi, ham_lo[:, cols]) + dot(lo, top) + dot(hi, top)
            value = value.reshape(TILE // ROWS // 2, 2, ROWS, TILE)
            pairs = pl.ds(k * (TILE // ROWS // 2), TILE // ROWS // 2)
            acc[pairs, 0, :, cols] = acc[pairs, 0, :, cols] - value[:, 1]
            acc[pairs, 1, :, cols] = acc[pairs, 1, :, cols] + value[:, 0]

        each(0, N // TILE, columns)

    def decay(a):
        rate = damping[a]
        first, second = panels[2 * a], panels[2 * a + 1]
        acc[a, 0] = -(rate * first)
        acc[a, 1] = -(rate * second)
        pool[2 * a] = first
        pool[2 * a + 1] = second

    each(0, OWN, decay)

    lane = lax.broadcasted_iota(jnp.int32, (ROWS, N), 1)
    diagonal = lane == lax.broadcasted_iota(jnp.int32, (ROWS, N), 0) + r * ROWS
    for k in range(BATH):
        columns = jnp.broadcast_to(modes[k : k + 1, :], (ROWS, N))
        row_part = jnp.sum(jnp.where(diagonal, columns, 0.0), axis=1, keepdims=True)
        gap[k] = row_part - columns
        total[k] = row_part + columns

    forward_in(0)
    take_low(0)
    take_high(0)
    for k in (1, 3, 2):
        wait_bytes(low_part(k, c), h3_recv.at[k - 1])
        to_core(low_part(k, c), k)
        wait_bytes(high_part(k, c), h3_recv.at[k + 2])
        to_core(high_part(k, c), GROUPS + k)
    for k in (1, 2, 3):
        remote(
            picked.at[k - 1], pool.at[pl.ds(MATS + (k - 1) * 2 * CAP, 2 * CAP)],
            pick_send.at[k - 1], pick_recv.at[k - 1], (h + k) % GROUPS, r,
        ).start()
    for k in (1, 3, 2):
        take_low(k)
        take_high(k)
    forward_in(1)
    multiply_left(0)
    multiply_left(1)
    forward_back(0)
    forward_in(2)
    forward_back(1)
    forward_in(3)
    multiply_left(2)
    multiply_left(3)
    forward_back(2)
    forward_back(3)
    each(0, MATS * ROWS // TILE, multiply_right)

    for d in range(1, GROUPS):
        wait_bytes(pool.at[pl.ds(MATS + (d - 1) * 2 * CAP, 2 * CAP)], pick_recv.at[d - 1])
    names = []
    for d in range(1, GROUPS):
        names += sorted_links(links_vec, h, (h + GROUPS - d) % GROUPS)

    def couple(a):
        real, imag = acc[a, 0], acc[a, 1]
        for slot in range(SLOTS):
            link = links[slot, h * OWN + a]
            mode = bath[slot, h * OWN + a]
            kind = kinds[slot, h * OWN + a]
            place = link - h * OWN
            for i, name in enumerate(names):
                place = jnp.where(link == name, OWN + i, place)
            direct = jnp.where(kind == 1, 1.0, jnp.where(kind == 2, coeff[0, mode], 0.0))
            mixing = jnp.where(kind == 2, coeff[1, mode], 0.0)
            first, second = pool[2 * place], pool[2 * place + 1]
            across = direct * gap[mode]
            along = mixing * total[mode]
            real = real + (across * second + along * first)
            imag = imag + (along * second - across * first)
        acc[a, 0], acc[a, 1] = real, imag

    each(0, OWN, couple)

    for j in range(CHUNKS):
        cols = pl.ds(j * WIDE, WIDE)
        wait_bytes(z_back.at[j], zb_recv.at[j])

        def finish(k, j=j, cols=cols):
            part = pl.ds(k * 2, 2)
            back = z_back[j, pl.ds(k * 4, 4)].reshape(2, 2, ROWS, WIDE)
            real = acc[part, 0, :, cols] + back[:, 1]
            imag = acc[part, 1, :, cols] - back[:, 0]
            acc[part, 0, :, cols] = real
            acc[part, 1, :, cols] = imag
            new[part, 0, :, cols] = new[part, 0, :, cols] + third_step * real
            new[part, 1, :, cols] = new[part, 1, :, cols] + third_step * imag

        each(0, OWN // 2, finish)

    wait_bytes(ham_buf.at[0, 0, pl.ds(0, ZS - 1), 0], h1_send)
    wait_bytes(ham_buf.at[0, 0, low, pl.ds(0, YS - 1)], h2_send.at[0])
    wait_bytes(ham_buf.at[0, 0, high, pl.ds(0, YS - 1)], h2_send.at[1])
    for k in range(2 * GROUPS - 2):
        wait_bytes(ham_buf.at[0, 0, low], h3_send.at[k])
    for k in range(2 * GROUPS):
        wait_bytes(ham_buf.at[0, 0, low], h4_send.at[k])
    for k in range(GROUPS - 1):
        wait_bytes(picked.at[0], pick_send.at[k])
    for j in range(CHUNKS):
        wait_bytes(z_in.at[0, pl.ds(0, ZS - 1)], zi_send.at[j])
        wait_bytes(y_in.at[0, :, pl.ds(0, YC - 1)], yi_send.at[j])
        wait_bytes(left.at[0, :, pl.ds(0, YC - 1)], yb_send.at[j])
        wait_bytes(y_back.at[0, pl.ds(0, ZS - 1)], zb_send.at[j])


def section(*arrays):
    f32, bf16, i32 = jnp.float32, jnp.bfloat16, jnp.int32
    dma = pltpu.SemaphoreType.DMA
    four = (CHUNKS,)
    outs = [pltpu.VMEM((OWN, 2, ROWS, N), f32)] * 2
    return pl.pallas_call(
        kernel,
        out_shape=outs,
        in_specs=[pl.BlockSpec(memory_space=pltpu.HBM)] * len(arrays),
        out_specs=[pl.BlockSpec(memory_space=pltpu.VMEM)] * 2,
        scratch_shapes=[
            pltpu.VMEM((ROWS, N), f32),
            pltpu.VMEM((BATH, N), f32),
            pltpu.SMEM((2, BATH), f32),
            pltpu.SMEM((OWN,), f32),
            pltpu.VMEM((SLOTS, GROUPS * OWN), i32),
            pltpu.SMEM((SLOTS, GROUPS * OWN), i32),
            pltpu.SMEM((SLOTS, GROUPS * OWN), i32),
            pltpu.SMEM((SLOTS, GROUPS * OWN), i32),
            pltpu.VMEM((MATS, ROWS, N), f32),
            pltpu.VMEM((MATS, ROWS, N), f32),
            pltpu.VMEM((MATS, ROWS, N), f32),
            pltpu.VMEM((GROUPS, 2, ZS, YS, ROWS, QUART), f32),
            pltpu.VMEM((N, N), bf16),
            pltpu.VMEM((N, N), bf16),
            pltpu.VMEM((CHUNKS, ZS, YS, ROWS, WIDE), f32),
            pltpu.VMEM((CHUNKS, ZS, YC, ROWS, HALF), f32),
            pltpu.VMEM((N, WIDE), bf16),
            pltpu.VMEM((CHUNKS, ZS, YC, ROWS, HALF), f32),
            pltpu.VMEM((CHUNKS, ZS, YS, ROWS, WIDE), f32),
            pltpu.VMEM((CHUNKS, MATS, ROWS, WIDE), f32),
            pltpu.VMEM((MATS + (GROUPS - 1) * 2 * CAP, ROWS, N), f32),
            pltpu.VMEM((GROUPS - 1, 2 * CAP, ROWS, N), f32),
            pltpu.VMEM((BATH, ROWS, N), f32),
            pltpu.VMEM((BATH, ROWS, N), f32),
            pltpu.SemaphoreType.REGULAR, pltpu.SemaphoreType.REGULAR,
            dma(four), dma(four), dma((9,)),
            dma, dma, dma((2,)), dma((2,)),
            dma((6,)), dma((6,)), dma((8,)), dma((8,)),
            dma(four), dma(four), dma(four), dma(four),
            dma(four), dma(four), dma(four), dma(four),
            dma((3,)), dma((3,)),
        ],
        compiler_params=pltpu.CompilerParams(
            collective_id=0, has_side_effects=True, vmem_limit_bytes=48 * 1024 * 1024
        ),
        cost_estimate=pl.CostEstimate(flops=6 * 2**30, bytes_accessed=6 * 2**20, transcendentals=0),
        name="section",
    )(*[pltpu.with_memory_space_constraint(array, pltpu.HBM) for array in arrays])


def store_kernel(deriv, new, deriv_out, new_out, sem):
    copies = []
    for i in range(PIECES):
        part = pl.ds(i * (OWN // PIECES), OWN // PIECES)
        copies.append(pltpu.make_async_copy(deriv.at[part], deriv_out.at[part], sem.at[0, i]))
        copies.append(pltpu.make_async_copy(new.at[part], new_out.at[part], sem.at[1, i]))
    for copy in copies:
        copy.start()
    for copy in copies:
        copy.wait()


def store(deriv, new):
    shape = jax.ShapeDtypeStruct(deriv.shape, deriv.dtype)
    return pl.pallas_call(
        store_kernel,
        out_shape=[shape] * 2,
        in_specs=[pl.BlockSpec(memory_space=pltpu.VMEM)] * 2,
        out_specs=[pl.BlockSpec(memory_space=pltpu.HBM)] * 2,
        scratch_shapes=[pltpu.SemaphoreType.DMA((2, PIECES))],
        compiler_params=pltpu.CompilerParams(vmem_limit_bytes=8 * 1024 * 1024),
        cost_estimate=pl.CostEstimate(flops=0, bytes_accessed=4 * 2**20, transcendentals=0),
        name="store",
    )(*[pltpu.with_memory_space_constraint(array, pltpu.VMEM) for array in (deriv, new)])


def local(rho, incr, accum, ham, modes, coeff, damping, links, bath, kinds):
    deriv, new = section(
        rho.reshape(MATS, ROWS, N), incr.reshape(MATS, ROWS, N), accum, ham, modes, coeff, damping,
        links.T, bath.T, kinds.T,
    )
    return store(deriv, new)


def solution(mesh):
    in_specs = (
        P("hier", None, "row", None),
        P("hier", None, "row", None),
        P("hier", None, "row", None),
        P("row", None),
        P(),
        P(),
        P("hier"),
        P(),
        P(),
        P(),
    )
    out_specs = (P("hier", None, "row", None), P("hier", None, "row", None))
    return jax.shard_map(local, mesh=mesh, in_specs=in_specs, out_specs=out_specs, check_vma=False)
```

```python
import jax
import jax.numpy as jnp
from jax import lax
from jax.experimental import pallas as pl
from jax.experimental.pallas import tpu as pltpu
from jax.sharding import PartitionSpec as P

half_step = 0.1
third_step = 0.2 / 3.0

MESH = pl.DeviceIdType.MESH
GROUPS = 4
ZS = 8
YS = 4
YC = 8
OWN = 16
CAP = 4
MATS = 32
ROWS = 16
N = 1024
BATH = 8
SLOTS = 4
CHUNKS = 4
WIDE = N // CHUNKS
HALF = WIDE // 2
QUART = N // GROUPS
TILE = 256
PIECES = 4
LOW = 4
SPLIT = 4


def split(x):
    hi = x.astype(jnp.bfloat16)
    return hi, (x - hi.astype(jnp.float32)).astype(jnp.bfloat16)


def dot(a, b):
    return jnp.dot(a, b, preferred_element_type=jnp.float32)


def sorted_links(links_vec, rows_of, target):
    block = links_vec[...]
    member = lax.broadcasted_iota(jnp.int32, block.shape, 1) - rows_of * OWN
    mine = (member >= 0) & (member < OWN)
    low = target * OWN
    found, last = [], low - 1
    for _ in range(CAP):
        inside = mine & (block > last) & (block < low + OWN)
        last = jnp.minimum(jnp.min(jnp.where(inside, block, low + OWN - 1)), low + OWN - 1)
        found.append(last)
    return found


def kernel(
    rho, incr, accum, ham_hbm, modes_hbm, coeff_hbm, damping_hbm, links_hbm, bath_hbm, kinds_hbm,
    acc, new,
    ham, modes, coeff, damping, links_vec, links, bath, kinds,
    panels, rho_buf, incr_buf, ham_buf, ham_hi, ham_lo, z_in, y_in, right_cat, left, y_back, z_back,
    pool, picked, gap, total,
    line_sem, across_sem, rho_sem, incr_sem, load_sem, h1_send, h1_recv, h2_send, h2_recv, h3_send, h3_recv, h4_send, h4_recv,
    zi_send, zi_recv, yi_send, yi_recv, yb_send, yb_recv, zb_send, zb_recv, pick_send, pick_recv,
):
    h = lax.axis_index("hier")
    r = lax.axis_index("row")
    z = r // YC
    yc = r % YC
    y = yc // 2
    c = yc % 2

    def remote(src, dst, send, recv, group, row):
        return pltpu.make_async_remote_copy(
            src_ref=src, dst_ref=dst, send_sem=send, recv_sem=recv,
            device_id=(group, row), device_id_type=MESH,
        )

    def wait_bytes(ref, sem):
        pltpu.make_async_copy(ref, ref, sem).wait()

    def other_z(k):
        there = (z + ZS // 2 + k // 2 * (2 * (k % 2) - 1) + ZS) % ZS
        return there, there * YC + yc

    def other_yc(k):
        there = (yc + k) % YC
        return there, z * YC + there

    def each(first, last, body):
        def step(k, carry):
            body(k)
            return carry

        lax.fori_loop(first, last, step, 0)

    def load_panel(j):
        part = (slice(None), slice(None), pl.ds(j * WIDE, WIDE))
        return (
            pltpu.make_async_copy(rho.at[part], rho_buf.at[part], rho_sem.at[j]),
            pltpu.make_async_copy(incr.at[part], incr_buf.at[part], incr_sem.at[j]),
        )

    pairs = [
        (ham_hbm, ham), (modes_hbm, modes), (coeff_hbm, coeff), (damping_hbm, damping), (links_hbm, links_vec),
        (links_hbm, links), (bath_hbm, bath), (kinds_hbm, kinds), (accum, new),
    ]
    loads = [pltpu.make_async_copy(src, dst, load_sem.at[i]) for i, (src, dst) in enumerate(pairs)]
    loads[0].start()
    for load in load_panel(0):
        load.start()
    barrier = pltpu.get_barrier_semaphore()

    def greet(group, row):
        pl.semaphore_signal(barrier, inc=1, device_id=(group, row), device_id_type=MESH)

    def across(body):
        each(1, YC, lambda k: body(h, other_yc(k)[1]))
        each(1, GROUPS, lambda k: body((h + k) % GROUPS, r))

    each(1, ZS, lambda k: greet(h, other_z(k)[1]))

    @pl.when(z == 0)
    def _():
        across(greet)


    def make_panels(j):
        for load in load_panel(j):
            load.wait()
        cols = pl.ds(j * WIDE, WIDE)

        def make(m):
            part = pl.ds(m * 8, 8)
            panels[part, :, cols] = rho_buf[part, :, cols] + half_step * incr_buf[part, :, cols]

        each(0, MATS // 8, make)

    loads[0].wait()

    @pl.when(z == 0)
    def _():
        pl.semaphore_wait(barrier, ZS - 1 + YC - 1 + GROUPS - 1)

    @pl.when(z != 0)
    def _():
        pl.semaphore_wait(barrier, ZS - 1)


    ham_own = ham.at[:, pl.ds(pl.multiple_of(h * QUART, QUART), QUART)]

    def ham_along(source, part, offset, sem):
        dst = ham_buf.at[h, c, source, y]
        remote(part, dst, h1_send, h1_recv.at[sem], h, (z + offset + ZS) % ZS * YC + yc).start()

    pltpu.make_async_copy(ham_own, ham_buf.at[h, c, z, y], h1_recv.at[2]).start()
    ham_along(z, ham_own, 2, 0)
    ham_along(z, ham_own, -2, 1)
    ham_along(z, ham_own, 1, 2)
    ham_along(z, ham_own, -1, 2)

    def start_chunk(j, first=1, last=ZS):
        cols = pl.ds(j * WIDE, WIDE)

        def send_z(k):
            there, row = other_z(k)
            remote(
                panels.at[pl.ds(there * YS, YS), :, cols], z_in.at[j, z], zi_send.at[j], zi_recv.at[j], h, row
            ).start()

        if first == 1:
            make_panels(j)
            pltpu.make_async_copy(panels.at[pl.ds(z * YS, YS), :, cols], z_in.at[j, z], zi_recv.at[j]).start()
        each(first, last, send_z)

    start_chunk(0, 1, SPLIT)

    def signal(sem, group, row):
        pl.semaphore_signal(sem, inc=1, device_id=(group, row), device_id_type=MESH)

    @pl.when(z == 0)
    def _():
        across(lambda group, row: signal(line_sem, group, row))

    for j in range(1, CHUNKS):
        for load in load_panel(j):
            load.start()
    for load in loads[1:]:
        load.start()

    before, behind = (z + ZS - 2) % ZS, (z + 2) % ZS
    wait_bytes(ham_buf.at[h, c, before, y], h1_recv.at[0])
    wait_bytes(ham_buf.at[h, c, behind, y], h1_recv.at[1])
    ham_along(before, ham_buf.at[h, c, before, y], 1, 2)
    ham_along(behind, ham_buf.at[h, c, behind, y], -1, 2)
    ham_along(before, ham_buf.at[h, c, before, y], 2, 2)

    start_chunk(0, SPLIT, ZS)
    for j in range(1, CHUNKS):
        start_chunk(j)

    @pl.when(z == 0)
    def _():
        pl.semaphore_wait(line_sem, YC - 1 + GROUPS - 1)
        each(1, ZS, lambda k: signal(across_sem, h, other_z(k)[1]))

    @pl.when(z != 0)
    def _():
        pl.semaphore_wait(across_sem, 1)

    wait_bytes(ham_buf.at[h, c, pl.ds(0, ZS - 2), y], h1_recv.at[2])
    low, high = pl.ds(0, LOW), pl.ds(LOW, ZS - LOW)

    def y_row(k):
        return z * YC + (y + k) % YS * 2 + c

    for k in (1, 3, 2):
        part = ham_buf.at[h, c, low, y]
        remote(part, part, h2_send.at[0], h2_recv.at[0], h, y_row(k)).start()
        part = ham_buf.at[h, c, high, y]
        remote(part, part, h2_send.at[1], h2_recv.at[1], (h + k) % GROUPS, r).start()

    def low_on(y_from):
        part = ham_buf.at[h, c, low, y_from]
        for k in (1, 3, 2):
            remote(part, part, h3_send.at[k - 1], h3_recv.at[k - 1], (h + k) % GROUPS, r).start()

    def high_on(group):
        part = ham_buf.at[group, c, high, y]
        for k in (1, 3, 2):
            remote(part, part, h3_send.at[k + 2], h3_recv.at[k + 2], h, y_row(k)).start()

    low_on(y)
    high_on(h)
    for load in loads[1:]:
        load.wait()

    for d in range(1, GROUPS):
        chosen = sorted_links(links_vec, (h + d) % GROUPS, h)
        for i in range(CAP):
            place = (chosen[i] - h * OWN) * 2
            picked[d - 1, 2 * i] = panels[place]
            picked[d - 1, 2 * i + 1] = panels[place + 1]

    def low_part(k, core):
        return ham_buf.at[(h + GROUPS - k) % GROUPS, core, low]

    def high_part(k, core):
        return ham_buf.at[:, core, high, (y + YS - k) % YS]

    def to_core(part, i):
        remote(part, part, h4_send.at[i], h4_recv.at[i], h, r - c + 1 - c).start()

    wait_bytes(ham_buf.at[h, c, low, pl.ds(0, YS - 1)], h2_recv.at[0])
    for k in (1, 3, 2):
        low_on((y + k) % YS)
    wait_bytes(ham_buf.at[pl.ds(0, GROUPS - 1), c, high, y], h2_recv.at[1])
    for k in (1, 3, 2):
        high_on((h + k) % GROUPS)
    to_core(low_part(0, c), 0)
    to_core(high_part(0, c), GROUPS)

    def forward_in(j):
        wait_bytes(z_in.at[j], zi_recv.at[j])

        def send_y(k):
            there, row = other_yc(k)
            remote(
                z_in.at[j, :, there // 2, :, pl.ds(pl.multiple_of(there % 2 * HALF, HALF), HALF)],
                y_in.at[j, :, yc], yi_send.at[j], yi_recv.at[j], h, row,
            ).start()

        pltpu.make_async_copy(
            z_in.at[j, :, y, :, pl.ds(pl.multiple_of(c * HALF, HALF), HALF)], y_in.at[j, :, yc], yi_recv.at[j]
        ).start()
        each(1, YC, send_y)

    def take(q, k):
        cols = pl.ds(pl.multiple_of(q * QUART, QUART), QUART)
        for cc in range(2):
            hi, lo = split(ham_buf[q, cc, k // YS, k % YS])
            rows = pl.ds(pl.multiple_of((k * 2 + cc) * ROWS, ROWS), ROWS)
            ham_hi[rows, cols] = hi
            ham_lo[rows, cols] = lo

    def take_low(k):
        wait_bytes(low_part(k, 1 - c), h4_recv.at[k])
        q = (h + GROUPS - k) % GROUPS
        each(0, LOW * YS, lambda i: take(q, i))

    def take_high(k):
        wait_bytes(high_part(k, 1 - c), h4_recv.at[GROUPS + k])
        yy = (y + YS - k) % YS
        each(0, (ZS - LOW) * GROUPS, lambda i: take(i // (ZS - LOW), (LOW + i % (ZS - LOW)) * YS + yy))

    def multiply_left(j):
        wait_bytes(y_in.at[j], yi_recv.at[j])

        def cut(k):
            hi, lo = split(y_in[j, k].reshape(YC * ROWS, HALF))
            rows = pl.ds(pl.multiple_of(k * YC * ROWS, YC * ROWS), YC * ROWS)
            right_cat[rows, 0:HALF] = hi
            right_cat[rows, HALF:WIDE] = lo

        each(0, ZS, cut)

        def half(i):
            def rows_of(ref):
                starts = [(z + 2 + i * (ZS // 2) + k) % ZS * (YC * ROWS) for k in range(ZS // 2)]
                return jnp.concatenate([ref[pl.ds(pl.multiple_of(at, YC * ROWS), YC * ROWS), :] for at in starts], axis=0)

            both = dot(rows_of(ham_hi), right_cat[...])
            value = both[:, HALF:] + dot(rows_of(ham_lo), right_cat[:, 0:HALF]) + both[:, :HALF]
            part = pl.ds(i * (ZS // 2), ZS // 2)
            left[j, part] = value.reshape(ZS // 2, YC, ROWS, HALF)
            dst = y_back.at[j, part, y, :, pl.ds(pl.multiple_of(c * HALF, HALF), HALF)]

            def send_y(k):
                there, row = other_yc(k)
                remote(left.at[j, part, there], dst, yb_send.at[j], yb_recv.at[j, i], h, row).start()

            pltpu.make_async_copy(left.at[j, part, yc], dst, yb_recv.at[j, i]).start()
            each(1, YC, send_y)

        each(0, 2, half)

    def forward_back(j):
        def send_z(place):
            there = (z + 2 + place) % ZS
            remote(
                y_back.at[j, place], z_back.at[j, pl.ds(z * YS, YS)], zb_send.at[j], zb_recv.at[j], h,
                there * YC + yc,
            ).start()

        wait_bytes(y_back.at[j, pl.ds(0, ZS // 2)], yb_recv.at[j, 0])
        for place in (2, 1, 3, 0):
            send_z(place)
        wait_bytes(y_back.at[j, pl.ds(ZS // 2, ZS // 2)], yb_recv.at[j, 1])
        pltpu.make_async_copy(y_back.at[j, ZS - 2], z_back.at[j, pl.ds(z * YS, YS)], zb_recv.at[j]).start()
        for place in (4, 7, 5):
            send_z(place)

    def multiply_right(k):
        rows = pl.ds(k * (TILE // ROWS), TILE // ROWS)
        hi, lo = split(panels[rows].reshape(TILE, N))

        def columns(q):
            cols = pl.ds(pl.multiple_of(q * TILE, TILE), TILE)
            top = ham_hi[:, cols]
            value = dot(hi, ham_lo[:, cols]) + dot(lo, top) + dot(hi, top)
            value = value.reshape(TILE // ROWS // 2, 2, ROWS, TILE)
            pairs = pl.ds(k * (TILE // ROWS // 2), TILE // ROWS // 2)
            acc[pairs, 0, :, cols] = acc[pairs, 0, :, cols] - value[:, 1]
            acc[pairs, 1, :, cols] = acc[pairs, 1, :, cols] + value[:, 0]

        each(0, N // TILE, columns)

    def decay(a):
        rate = damping[a]
        first, second = panels[2 * a], panels[2 * a + 1]
        acc[a, 0] = -(rate * first)
        acc[a, 1] = -(rate * second)
        pool[2 * a] = first
        pool[2 * a + 1] = second

    each(0, OWN, decay)

    lane = lax.broadcasted_iota(jnp.int32, (ROWS, N), 1)
    diagonal = lane == lax.broadcasted_iota(jnp.int32, (ROWS, N), 0) + r * ROWS
    for k in range(BATH):
        columns = jnp.broadcast_to(modes[k : k + 1, :], (ROWS, N))
        row_part = jnp.sum(jnp.where(diagonal, columns, 0.0), axis=1, keepdims=True)
        gap[k] = row_part - columns
        total[k] = row_part + columns

    forward_in(0)
    take_low(0)
    take_high(0)
    for k in (1, 3, 2):
        wait_bytes(low_part(k, c), h3_recv.at[k - 1])
        to_core(low_part(k, c), k)
        wait_bytes(high_part(k, c), h3_recv.at[k + 2])
        to_core(high_part(k, c), GROUPS + k)
    for k in (1, 2, 3):
        remote(
            picked.at[k - 1], pool.at[pl.ds(MATS + (k - 1) * 2 * CAP, 2 * CAP)],
            pick_send.at[k - 1], pick_recv.at[k - 1], (h + k) % GROUPS, r,
        ).start()
    forward_in(1)
    for k in (1, 3, 2):
        take_low(k)
        take_high(k)
    multiply_left(0)
    multiply_left(1)
    forward_back(0)
    forward_in(2)
    forward_back(1)
    forward_in(3)
    multiply_left(2)
    multiply_left(3)
    forward_back(2)
    forward_back(3)
    each(0, MATS * ROWS // TILE, multiply_right)

    for d in range(1, GROUPS):
        wait_bytes(pool.at[pl.ds(MATS + (d - 1) * 2 * CAP, 2 * CAP)], pick_recv.at[d - 1])
    names = []
    for d in range(1, GROUPS):
        names += sorted_links(links_vec, h, (h + GROUPS - d) % GROUPS)

    def couple(a):
        real, imag = acc[a, 0], acc[a, 1]
        for slot in range(SLOTS):
            link = links[slot, h * OWN + a]
            mode = bath[slot, h * OWN + a]
            kind = kinds[slot, h * OWN + a]
            place = link - h * OWN
            for i, name in enumerate(names):
                place = jnp.where(link == name, OWN + i, place)
            direct = jnp.where(kind == 1, 1.0, jnp.where(kind == 2, coeff[0, mode], 0.0))
            mixing = jnp.where(kind == 2, coeff[1, mode], 0.0)
            first, second = pool[2 * place], pool[2 * place + 1]
            across = direct * gap[mode]
            along = mixing * total[mode]
            real = real + (across * second + along * first)
            imag = imag + (along * second - across * first)
        acc[a, 0], acc[a, 1] = real, imag

    each(0, OWN, couple)

    for j in range(CHUNKS):
        cols = pl.ds(j * WIDE, WIDE)
        wait_bytes(z_back.at[j], zb_recv.at[j])

        def finish(k, j=j, cols=cols):
            part = pl.ds(k * 2, 2)
            back = z_back[j, pl.ds(k * 4, 4)].reshape(2, 2, ROWS, WIDE)
            real = acc[part, 0, :, cols] + back[:, 1]
            imag = acc[part, 1, :, cols] - back[:, 0]
            acc[part, 0, :, cols] = real
            acc[part, 1, :, cols] = imag
            new[part, 0, :, cols] = new[part, 0, :, cols] + third_step * real
            new[part, 1, :, cols] = new[part, 1, :, cols] + third_step * imag

        each(0, OWN // 2, finish)

    wait_bytes(ham_buf.at[0, 0, pl.ds(0, ZS - 1), 0], h1_send)
    wait_bytes(ham_buf.at[0, 0, low, pl.ds(0, YS - 1)], h2_send.at[0])
    wait_bytes(ham_buf.at[0, 0, high, pl.ds(0, YS - 1)], h2_send.at[1])
    for k in range(GROUPS - 1):
        wait_bytes(low_part(0, 0), h3_send.at[k])
        wait_bytes(high_part(0, 0), h3_send.at[GROUPS - 1 + k])
    for k in range(GROUPS):
        wait_bytes(low_part(0, 0), h4_send.at[k])
        wait_bytes(high_part(0, 0), h4_send.at[GROUPS + k])
    for k in range(GROUPS - 1):
        wait_bytes(picked.at[0], pick_send.at[k])
    for j in range(CHUNKS):
        wait_bytes(z_in.at[0, pl.ds(0, ZS - 1)], zi_send.at[j])
        wait_bytes(y_in.at[0, :, pl.ds(0, YC - 1)], yi_send.at[j])
        wait_bytes(left.at[0, :, pl.ds(0, YC - 1)], yb_send.at[j])
        wait_bytes(y_back.at[0, pl.ds(0, ZS - 1)], zb_send.at[j])


def section(*arrays):
    f32, bf16, i32 = jnp.float32, jnp.bfloat16, jnp.int32
    dma = pltpu.SemaphoreType.DMA
    four = (CHUNKS,)
    outs = [pltpu.VMEM((OWN, 2, ROWS, N), f32)] * 2
    return pl.pallas_call(
        kernel,
        out_shape=outs,
        in_specs=[pl.BlockSpec(memory_space=pltpu.HBM)] * len(arrays),
        out_specs=[pl.BlockSpec(memory_space=pltpu.VMEM)] * 2,
        scratch_shapes=[
            pltpu.VMEM((ROWS, N), f32),
            pltpu.VMEM((BATH, N), f32),
            pltpu.SMEM((2, BATH), f32),
            pltpu.SMEM((OWN,), f32),
            pltpu.VMEM((SLOTS, GROUPS * OWN), i32),
            pltpu.SMEM((SLOTS, GROUPS * OWN), i32),
            pltpu.SMEM((SLOTS, GROUPS * OWN), i32),
            pltpu.SMEM((SLOTS, GROUPS * OWN), i32),
            pltpu.VMEM((MATS, ROWS, N), f32),
            pltpu.VMEM((MATS, ROWS, N), f32),
            pltpu.VMEM((MATS, ROWS, N), f32),
            pltpu.VMEM((GROUPS, 2, ZS, YS, ROWS, QUART), f32),
            pltpu.VMEM((N, N), bf16),
            pltpu.VMEM((N, N), bf16),
            pltpu.VMEM((CHUNKS, ZS, YS, ROWS, WIDE), f32),
            pltpu.VMEM((CHUNKS, ZS, YC, ROWS, HALF), f32),
            pltpu.VMEM((N, WIDE), bf16),
            pltpu.VMEM((CHUNKS, ZS, YC, ROWS, HALF), f32),
            pltpu.VMEM((CHUNKS, ZS, YS, ROWS, WIDE), f32),
            pltpu.VMEM((CHUNKS, MATS, ROWS, WIDE), f32),
            pltpu.VMEM((MATS + (GROUPS - 1) * 2 * CAP, ROWS, N), f32),
            pltpu.VMEM((GROUPS - 1, 2 * CAP, ROWS, N), f32),
            pltpu.VMEM((BATH, ROWS, N), f32),
            pltpu.VMEM((BATH, ROWS, N), f32),
            pltpu.SemaphoreType.REGULAR, pltpu.SemaphoreType.REGULAR,
            dma(four), dma(four), dma((9,)),
            dma, dma((3,)), dma((2,)), dma((2,)),
            dma((6,)), dma((6,)), dma((8,)), dma((8,)),
            dma(four), dma(four), dma(four), dma(four),
            dma(four), dma((CHUNKS, 2)), dma(four), dma(four),
            dma((3,)), dma((3,)),
        ],
        compiler_params=pltpu.CompilerParams(
            collective_id=0, has_side_effects=True, vmem_limit_bytes=48 * 1024 * 1024
        ),
        cost_estimate=pl.CostEstimate(flops=6 * 2**30, bytes_accessed=6 * 2**20, transcendentals=0),
        name="section",
    )(*[pltpu.with_memory_space_constraint(array, pltpu.HBM) for array in arrays])


def store_kernel(deriv, new, deriv_out, new_out, sem):
    copies = []
    for i in range(PIECES):
        part = pl.ds(i * (OWN // PIECES), OWN // PIECES)
        copies.append(pltpu.make_async_copy(deriv.at[part], deriv_out.at[part], sem.at[0, i]))
        copies.append(pltpu.make_async_copy(new.at[part], new_out.at[part], sem.at[1, i]))
    for copy in copies:
        copy.start()
    for copy in copies:
        copy.wait()


def store(deriv, new):
    shape = jax.ShapeDtypeStruct(deriv.shape, deriv.dtype)
    return pl.pallas_call(
        store_kernel,
        out_shape=[shape] * 2,
        in_specs=[pl.BlockSpec(memory_space=pltpu.VMEM)] * 2,
        out_specs=[pl.BlockSpec(memory_space=pltpu.HBM)] * 2,
        scratch_shapes=[pltpu.SemaphoreType.DMA((2, PIECES))],
        compiler_params=pltpu.CompilerParams(vmem_limit_bytes=8 * 1024 * 1024),
        cost_estimate=pl.CostEstimate(flops=0, bytes_accessed=4 * 2**20, transcendentals=0),
        name="store",
    )(*[pltpu.with_memory_space_constraint(array, pltpu.VMEM) for array in (deriv, new)])


def local(rho, incr, accum, ham, modes, coeff, damping, links, bath, kinds):
    deriv, new = section(
        rho.reshape(MATS, ROWS, N), incr.reshape(MATS, ROWS, N), accum, ham, modes, coeff, damping,
        links.T, bath.T, kinds.T,
    )
    return store(deriv, new)


def solution(mesh):
    in_specs = (
        P("hier", None, "row", None),
        P("hier", None, "row", None),
        P("hier", None, "row", None),
        P("row", None),
        P(),
        P(),
        P("hier"),
        P(),
        P(),
        P(),
    )
    out_specs = (P("hier", None, "row", None), P("hier", None, "row", None))
    return jax.shard_map(local, mesh=mesh, in_specs=in_specs, out_specs=out_specs, check_vma=False)
```

```python
import jax
import jax.numpy as jnp
from jax import lax
from jax.experimental import pallas as pl
from jax.experimental.pallas import tpu as pltpu
from jax.sharding import PartitionSpec as P

half_step = 0.1
third_step = 0.2 / 3.0

MESH = pl.DeviceIdType.MESH
GROUPS = 4
ZS = 8
YS = 4
YC = 8
OWN = 16
CAP = 4
MATS = 32
ROWS = 16
N = 1024
BATH = 8
SLOTS = 4
CHUNKS = 4
WIDE = N // CHUNKS
HALF = WIDE // 2
QUART = N // GROUPS
TILE = 256
PIECES = 4
LOW = 4
SPLIT = 4


def split(x):
    hi = x.astype(jnp.bfloat16)
    return hi, (x - hi.astype(jnp.float32)).astype(jnp.bfloat16)


def dot(a, b):
    return jnp.dot(a, b, preferred_element_type=jnp.float32)


def sorted_links(links_vec, rows_of, target):
    block = links_vec[...]
    member = lax.broadcasted_iota(jnp.int32, block.shape, 1) - rows_of * OWN
    mine = (member >= 0) & (member < OWN)
    low = target * OWN
    found, last = [], low - 1
    for _ in range(CAP):
        inside = mine & (block > last) & (block < low + OWN)
        last = jnp.minimum(jnp.min(jnp.where(inside, block, low + OWN - 1)), low + OWN - 1)
        found.append(last)
    return found


def kernel(
    rho, incr, accum, ham_hbm, modes_hbm, coeff_hbm, damping_hbm, links_hbm, bath_hbm, kinds_hbm,
    acc, new,
    ham, modes, coeff, damping, links_vec, links, bath, kinds,
    panels, rho_buf, incr_buf, ham_buf, ham_hi, ham_lo, z_in, y_in, right_cat, left, y_back, z_back,
    pool, picked, gap, total,
    line_sem, across_sem, rho_sem, incr_sem, load_sem, h1_send, h1_recv, h2_send, h2_recv, h3_send, h3_recv, h4_send, h4_recv,
    zi_send, zi_recv, yi_send, yi_recv, yb_send, yb_recv, zb_send, zb_recv, pick_send, pick_recv,
):
    h = lax.axis_index("hier")
    r = lax.axis_index("row")
    z = r // YC
    yc = r % YC
    y = yc // 2
    c = yc % 2

    def remote(src, dst, send, recv, group, row):
        return pltpu.make_async_remote_copy(
            src_ref=src, dst_ref=dst, send_sem=send, recv_sem=recv,
            device_id=(group, row), device_id_type=MESH,
        )

    def wait_bytes(ref, sem):
        pltpu.make_async_copy(ref, ref, sem).wait()

    def other_z(k):
        there = (z + ZS // 2 + k // 2 * (2 * (k % 2) - 1) + ZS) % ZS
        return there, there * YC + yc

    def other_yc(k):
        there = (yc + k) % YC
        return there, z * YC + there

    def each(first, last, body):
        def step(k, carry):
            body(k)
            return carry

        lax.fori_loop(first, last, step, 0)

    def load_panel(j):
        part = (slice(None), slice(None), pl.ds(j * WIDE, WIDE))
        return (
            pltpu.make_async_copy(rho.at[part], rho_buf.at[part], rho_sem.at[j]),
            pltpu.make_async_copy(incr.at[part], incr_buf.at[part], incr_sem.at[j]),
        )

    pairs = [
        (ham_hbm, ham), (modes_hbm, modes), (coeff_hbm, coeff), (damping_hbm, damping), (links_hbm, links_vec),
        (links_hbm, links), (bath_hbm, bath), (kinds_hbm, kinds), (accum, new),
    ]
    loads = [pltpu.make_async_copy(src, dst, load_sem.at[i]) for i, (src, dst) in enumerate(pairs)]
    barrier = pltpu.get_barrier_semaphore()

    def greet(group, row):
        pl.semaphore_signal(barrier, inc=1, device_id=(group, row), device_id_type=MESH)

    def across(body):
        each(1, YC, lambda k: body(h, other_yc(k)[1]))
        each(1, GROUPS, lambda k: body((h + k) % GROUPS, r))

    each(1, ZS, lambda k: greet(h, other_z(k)[1]))
    loads[0].start()
    for load in load_panel(0):
        load.start()

    @pl.when(z == 0)
    def _():
        across(greet)


    def make_panels(j):
        for load in load_panel(j):
            load.wait()
        cols = pl.ds(j * WIDE, WIDE)

        def make(m):
            part = pl.ds(m * 8, 8)
            panels[part, :, cols] = rho_buf[part, :, cols] + half_step * incr_buf[part, :, cols]

        each(0, MATS // 8, make)

    loads[0].wait()

    @pl.when(z == 0)
    def _():
        pl.semaphore_wait(barrier, ZS - 1 + YC - 1 + GROUPS - 1)

    @pl.when(z != 0)
    def _():
        pl.semaphore_wait(barrier, ZS - 1)


    ham_own = ham.at[:, pl.ds(pl.multiple_of(h * QUART, QUART), QUART)]

    turn = 1 - 2 * c

    def ham_along(source, part, offset, sem):
        dst = ham_buf.at[h, c, source, y]
        remote(part, dst, h1_send, h1_recv.at[sem], h, (z + offset * turn + ZS) % ZS * YC + yc).start()

    pltpu.make_async_copy(ham_own, ham_buf.at[h, c, z, y], h1_recv.at[2]).start()
    ham_along(z, ham_own, 2, 0)
    ham_along(z, ham_own, -2, 1)
    ham_along(z, ham_own, 1, 2)
    ham_along(z, ham_own, -1, 2)

    def start_chunk(j, first=1, last=ZS):
        cols = pl.ds(j * WIDE, WIDE)

        def send_z(k):
            there, row = other_z(k)
            remote(
                panels.at[pl.ds(there * YS, YS), :, cols], z_in.at[j, z], zi_send.at[j], zi_recv.at[j], h, row
            ).start()

        if first == 1:
            make_panels(j)
            pltpu.make_async_copy(panels.at[pl.ds(z * YS, YS), :, cols], z_in.at[j, z], zi_recv.at[j]).start()
        each(first, last, send_z)

    start_chunk(0, 1, SPLIT)

    def signal(sem, group, row):
        pl.semaphore_signal(sem, inc=1, device_id=(group, row), device_id_type=MESH)

    @pl.when(z == 0)
    def _():
        across(lambda group, row: signal(line_sem, group, row))

    for j in range(1, CHUNKS):
        for load in load_panel(j):
            load.start()
    for load in loads[1:]:
        load.start()

    before, behind = (z + ZS - 2 * turn) % ZS, (z + ZS + 2 * turn) % ZS
    wait_bytes(ham_buf.at[h, c, before, y], h1_recv.at[0])
    wait_bytes(ham_buf.at[h, c, behind, y], h1_recv.at[1])
    ham_along(before, ham_buf.at[h, c, before, y], 1, 2)
    ham_along(behind, ham_buf.at[h, c, behind, y], -1, 2)
    ham_along(before, ham_buf.at[h, c, before, y], 2, 2)

    start_chunk(0, SPLIT, ZS)
    for j in range(1, CHUNKS):
        start_chunk(j)

    @pl.when(z == 0)
    def _():
        pl.semaphore_wait(line_sem, YC - 1 + GROUPS - 1)
        each(1, ZS, lambda k: signal(across_sem, h, other_z(k)[1]))

    @pl.when(z != 0)
    def _():
        pl.semaphore_wait(across_sem, 1)

    wait_bytes(ham_buf.at[h, c, pl.ds(0, ZS - 2), y], h1_recv.at[2])
    low, high = pl.ds(0, LOW), pl.ds(LOW, ZS - LOW)

    def y_row(k):
        return z * YC + (y + k) % YS * 2 + c

    for k in (1, 3, 2):
        part = ham_buf.at[h, c, low, y]
        remote(part, part, h2_send.at[0], h2_recv.at[0], h, y_row(k)).start()
        part = ham_buf.at[h, c, high, y]
        remote(part, part, h2_send.at[1], h2_recv.at[1], (h + k) % GROUPS, r).start()

    def low_on(y_from):
        part = ham_buf.at[h, c, low, y_from]
        for k in (1, 3, 2):
            remote(part, part, h3_send.at[k - 1], h3_recv.at[k - 1], (h + k) % GROUPS, r).start()

    def high_on(group):
        part = ham_buf.at[group, c, high, y]
        for k in (1, 3, 2):
            remote(part, part, h3_send.at[k + 2], h3_recv.at[k + 2], h, y_row(k)).start()

    low_on(y)
    high_on(h)
    for load in loads[1:]:
        load.wait()

    for d in range(1, GROUPS):
        chosen = sorted_links(links_vec, (h + d) % GROUPS, h)
        for i in range(CAP):
            place = (chosen[i] - h * OWN) * 2
            picked[d - 1, 2 * i] = panels[place]
            picked[d - 1, 2 * i + 1] = panels[place + 1]

    def low_part(k, core):
        return ham_buf.at[(h + GROUPS - k) % GROUPS, core, low]

    def high_part(k, core):
        return ham_buf.at[:, core, high, (y + YS - k) % YS]

    def to_core(part, i):
        remote(part, part, h4_send.at[i], h4_recv.at[i], h, r - c + 1 - c).start()

    wait_bytes(ham_buf.at[h, c, low, pl.ds(0, YS - 1)], h2_recv.at[0])
    for k in (1, 3, 2):
        low_on((y + k) % YS)
    wait_bytes(ham_buf.at[pl.ds(0, GROUPS - 1), c, high, y], h2_recv.at[1])
    for k in (1, 3, 2):
        high_on((h + k) % GROUPS)
    to_core(low_part(0, c), 0)
    to_core(high_part(0, c), GROUPS)

    def forward_in(j):
        wait_bytes(z_in.at[j], zi_recv.at[j])

        def send_y(k):
            there, row = other_yc(k)
            remote(
                z_in.at[j, :, there // 2, :, pl.ds(pl.multiple_of(there % 2 * HALF, HALF), HALF)],
                y_in.at[j, :, yc], yi_send.at[j], yi_recv.at[j], h, row,
            ).start()

        pltpu.make_async_copy(
            z_in.at[j, :, y, :, pl.ds(pl.multiple_of(c * HALF, HALF), HALF)], y_in.at[j, :, yc], yi_recv.at[j]
        ).start()
        each(1, YC, send_y)

    def take(q, k):
        cols = pl.ds(pl.multiple_of(q * QUART, QUART), QUART)
        for cc in range(2):
            hi, lo = split(ham_buf[q, cc, k // YS, k % YS])
            rows = pl.ds(pl.multiple_of((k * 2 + cc) * ROWS, ROWS), ROWS)
            ham_hi[rows, cols] = hi
            ham_lo[rows, cols] = lo

    def take_low(k):
        wait_bytes(low_part(k, 1 - c), h4_recv.at[k])
        q = (h + GROUPS - k) % GROUPS
        each(0, LOW * YS, lambda i: take(q, i))

    def take_high(k):
        wait_bytes(high_part(k, 1 - c), h4_recv.at[GROUPS + k])
        yy = (y + YS - k) % YS
        each(0, (ZS - LOW) * GROUPS, lambda i: take(i // (ZS - LOW), (LOW + i % (ZS - LOW)) * YS + yy))

    def multiply_left(j):
        wait_bytes(y_in.at[j], yi_recv.at[j])

        def cut(k):
            hi, lo = split(y_in[j, k].reshape(YC * ROWS, HALF))
            rows = pl.ds(pl.multiple_of(k * YC * ROWS, YC * ROWS), YC * ROWS)
            right_cat[rows, 0:HALF] = hi
            right_cat[rows, HALF:WIDE] = lo

        each(0, ZS, cut)

        def half(i):
            def rows_of(ref):
                starts = [(z + 2 + i * (ZS // 2) + k) % ZS * (YC * ROWS) for k in range(ZS // 2)]
                return jnp.concatenate([ref[pl.ds(pl.multiple_of(at, YC * ROWS), YC * ROWS), :] for at in starts], axis=0)

            both = dot(rows_of(ham_hi), right_cat[...])
            value = both[:, HALF:] + dot(rows_of(ham_lo), right_cat[:, 0:HALF]) + both[:, :HALF]
            part = pl.ds(i * (ZS // 2), ZS // 2)
            left[j, part] = value.reshape(ZS // 2, YC, ROWS, HALF)
            dst = y_back.at[j, part, y, :, pl.ds(pl.multiple_of(c * HALF, HALF), HALF)]

            def send_y(k):
                there, row = other_yc(k)
                remote(left.at[j, part, there], dst, yb_send.at[j], yb_recv.at[j, i], h, row).start()

            pltpu.make_async_copy(left.at[j, part, yc], dst, yb_recv.at[j, i]).start()
            each(1, YC, send_y)

        each(0, 2, half)

    def forward_back(j):
        def send_z(place):
            there = (z + 2 + place) % ZS
            remote(
                y_back.at[j, place], z_back.at[j, pl.ds(z * YS, YS)], zb_send.at[j], zb_recv.at[j], h,
                there * YC + yc,
            ).start()

        wait_bytes(y_back.at[j, pl.ds(0, ZS // 2)], yb_recv.at[j, 0])
        for place in (2, 1, 3, 0):
            send_z(place)
        wait_bytes(y_back.at[j, pl.ds(ZS // 2, ZS // 2)], yb_recv.at[j, 1])
        pltpu.make_async_copy(y_back.at[j, ZS - 2], z_back.at[j, pl.ds(z * YS, YS)], zb_recv.at[j]).start()
        for place in (4, 7, 5):
            send_z(place)

    def multiply_right(k):
        rows = pl.ds(k * (TILE // ROWS), TILE // ROWS)
        hi, lo = split(panels[rows].reshape(TILE, N))

        def columns(q):
            cols = pl.ds(pl.multiple_of(q * TILE, TILE), TILE)
            top = ham_hi[:, cols]
            value = dot(hi, ham_lo[:, cols]) + dot(lo, top) + dot(hi, top)
            value = value.reshape(TILE // ROWS // 2, 2, ROWS, TILE)
            pairs = pl.ds(k * (TILE // ROWS // 2), TILE // ROWS // 2)
            acc[pairs, 0, :, cols] = acc[pairs, 0, :, cols] - value[:, 1]
            acc[pairs, 1, :, cols] = acc[pairs, 1, :, cols] + value[:, 0]

        each(0, N // TILE, columns)

    def decay(a):
        rate = damping[a]
        first, second = panels[2 * a], panels[2 * a + 1]
        acc[a, 0] = -(rate * first)
        acc[a, 1] = -(rate * second)
        pool[2 * a] = first
        pool[2 * a + 1] = second

    each(0, OWN, decay)

    lane = lax.broadcasted_iota(jnp.int32, (ROWS, N), 1)
    diagonal = lane == lax.broadcasted_iota(jnp.int32, (ROWS, N), 0) + r * ROWS
    for k in range(BATH):
        columns = jnp.broadcast_to(modes[k : k + 1, :], (ROWS, N))
        row_part = jnp.sum(jnp.where(diagonal, columns, 0.0), axis=1, keepdims=True)
        gap[k] = row_part - columns
        total[k] = row_part + columns

    forward_in(0)
    take_low(0)
    take_high(0)
    for k in (1, 3, 2):
        wait_bytes(low_part(k, c), h3_recv.at[k - 1])
        to_core(low_part(k, c), k)
        wait_bytes(high_part(k, c), h3_recv.at[k + 2])
        to_core(high_part(k, c), GROUPS + k)
    for k in (1, 2, 3):
        remote(
            picked.at[k - 1], pool.at[pl.ds(MATS + (k - 1) * 2 * CAP, 2 * CAP)],
            pick_send.at[k - 1], pick_recv.at[k - 1], (h + k) % GROUPS, r,
        ).start()
    forward_in(1)
    for k in (1, 3, 2):
        take_low(k)
        take_high(k)
    multiply_left(0)
    multiply_left(1)
    forward_back(0)
    forward_in(2)
    forward_back(1)
    forward_in(3)
    multiply_left(2)
    multiply_left(3)
    forward_back(2)
    forward_back(3)
    each(0, MATS * ROWS // TILE, multiply_right)

    for d in range(1, GROUPS):
        wait_bytes(pool.at[pl.ds(MATS + (d - 1) * 2 * CAP, 2 * CAP)], pick_recv.at[d - 1])
    names = []
    for d in range(1, GROUPS):
        names += sorted_links(links_vec, h, (h + GROUPS - d) % GROUPS)

    def couple(a):
        real, imag = acc[a, 0], acc[a, 1]
        for slot in range(SLOTS):
            link = links[slot, h * OWN + a]
            mode = bath[slot, h * OWN + a]
            kind = kinds[slot, h * OWN + a]
            place = link - h * OWN
            for i, name in enumerate(names):
                place = jnp.where(link == name, OWN + i, place)
            place = jnp.clip(place, 0, OWN + (GROUPS - 1) * CAP - 1)
            direct = jnp.where(kind == 1, 1.0, jnp.where(kind == 2, coeff[0, mode], 0.0))
            mixing = jnp.where(kind == 2, coeff[1, mode], 0.0)
            first, second = pool[2 * place], pool[2 * place + 1]
            across = direct * gap[mode]
            along = mixing * total[mode]
            real = real + (across * second + along * first)
            imag = imag + (along * second - across * first)
        acc[a, 0], acc[a, 1] = real, imag

    each(0, OWN, couple)

    for j in range(CHUNKS):
        cols = pl.ds(j * WIDE, WIDE)
        wait_bytes(z_back.at[j], zb_recv.at[j])

        def finish(k, j=j, cols=cols):
            part = pl.ds(k * 2, 2)
            back = z_back[j, pl.ds(k * 4, 4)].reshape(2, 2, ROWS, WIDE)
            real = acc[part, 0, :, cols] + back[:, 1]
            imag = acc[part, 1, :, cols] - back[:, 0]
            acc[part, 0, :, cols] = real
            acc[part, 1, :, cols] = imag
            new[part, 0, :, cols] = new[part, 0, :, cols] + third_step * real
            new[part, 1, :, cols] = new[part, 1, :, cols] + third_step * imag

        each(0, OWN // 2, finish)

    wait_bytes(ham_buf.at[0, 0, pl.ds(0, ZS - 1), 0], h1_send)
    wait_bytes(ham_buf.at[0, 0, low, pl.ds(0, YS - 1)], h2_send.at[0])
    wait_bytes(ham_buf.at[0, 0, high, pl.ds(0, YS - 1)], h2_send.at[1])
    for k in range(GROUPS - 1):
        wait_bytes(low_part(0, 0), h3_send.at[k])
        wait_bytes(high_part(0, 0), h3_send.at[GROUPS - 1 + k])
    for k in range(GROUPS):
        wait_bytes(low_part(0, 0), h4_send.at[k])
        wait_bytes(high_part(0, 0), h4_send.at[GROUPS + k])
    for k in range(GROUPS - 1):
        wait_bytes(picked.at[0], pick_send.at[k])
    for j in range(CHUNKS):
        wait_bytes(z_in.at[0, pl.ds(0, ZS - 1)], zi_send.at[j])
        wait_bytes(y_in.at[0, :, pl.ds(0, YC - 1)], yi_send.at[j])
        wait_bytes(left.at[0, :, pl.ds(0, YC - 1)], yb_send.at[j])
        wait_bytes(y_back.at[0, pl.ds(0, ZS - 1)], zb_send.at[j])


def section(*arrays):
    f32, bf16, i32 = jnp.float32, jnp.bfloat16, jnp.int32
    dma = pltpu.SemaphoreType.DMA
    four = (CHUNKS,)
    outs = [pltpu.VMEM((OWN, 2, ROWS, N), f32)] * 2
    return pl.pallas_call(
        kernel,
        out_shape=outs,
        in_specs=[pl.BlockSpec(memory_space=pltpu.HBM)] * len(arrays),
        out_specs=[pl.BlockSpec(memory_space=pltpu.VMEM)] * 2,
        scratch_shapes=[
            pltpu.VMEM((ROWS, N), f32),
            pltpu.VMEM((BATH, N), f32),
            pltpu.SMEM((2, BATH), f32),
            pltpu.SMEM((OWN,), f32),
            pltpu.VMEM((SLOTS, GROUPS * OWN), i32),
            pltpu.SMEM((SLOTS, GROUPS * OWN), i32),
            pltpu.SMEM((SLOTS, GROUPS * OWN), i32),
            pltpu.SMEM((SLOTS, GROUPS * OWN), i32),
            pltpu.VMEM((MATS, ROWS, N), f32),
            pltpu.VMEM((MATS, ROWS, N), f32),
            pltpu.VMEM((MATS, ROWS, N), f32),
            pltpu.VMEM((GROUPS, 2, ZS, YS, ROWS, QUART), f32),
            pltpu.VMEM((N, N), bf16),
            pltpu.VMEM((N, N), bf16),
            pltpu.VMEM((CHUNKS, ZS, YS, ROWS, WIDE), f32),
            pltpu.VMEM((CHUNKS, ZS, YC, ROWS, HALF), f32),
            pltpu.VMEM((N, WIDE), bf16),
            pltpu.VMEM((CHUNKS, ZS, YC, ROWS, HALF), f32),
            pltpu.VMEM((CHUNKS, ZS, YS, ROWS, WIDE), f32),
            pltpu.VMEM((CHUNKS, MATS, ROWS, WIDE), f32),
            pltpu.VMEM((MATS + (GROUPS - 1) * 2 * CAP, ROWS, N), f32),
            pltpu.VMEM((GROUPS - 1, 2 * CAP, ROWS, N), f32),
            pltpu.VMEM((BATH, ROWS, N), f32),
            pltpu.VMEM((BATH, ROWS, N), f32),
            pltpu.SemaphoreType.REGULAR, pltpu.SemaphoreType.REGULAR,
            dma(four), dma(four), dma((9,)),
            dma, dma((3,)), dma((2,)), dma((2,)),
            dma((6,)), dma((6,)), dma((8,)), dma((8,)),
            dma(four), dma(four), dma(four), dma(four),
            dma(four), dma((CHUNKS, 2)), dma(four), dma(four),
            dma((3,)), dma((3,)),
        ],
        compiler_params=pltpu.CompilerParams(
            collective_id=0, has_side_effects=True, vmem_limit_bytes=48 * 1024 * 1024
        ),
        cost_estimate=pl.CostEstimate(flops=6 * 2**30, bytes_accessed=6 * 2**20, transcendentals=0),
        name="section",
    )(*[pltpu.with_memory_space_constraint(array, pltpu.HBM) for array in arrays])


def store_kernel(deriv, new, deriv_out, new_out, sem):
    copies = []
    for i in range(PIECES):
        part = pl.ds(i * (OWN // PIECES), OWN // PIECES)
        copies.append(pltpu.make_async_copy(deriv.at[part], deriv_out.at[part], sem.at[0, i]))
        copies.append(pltpu.make_async_copy(new.at[part], new_out.at[part], sem.at[1, i]))
    for copy in copies:
        copy.start()
    for copy in copies:
        copy.wait()


def store(deriv, new):
    shape = jax.ShapeDtypeStruct(deriv.shape, deriv.dtype)
    return pl.pallas_call(
        store_kernel,
        out_shape=[shape] * 2,
        in_specs=[pl.BlockSpec(memory_space=pltpu.VMEM)] * 2,
        out_specs=[pl.BlockSpec(memory_space=pltpu.HBM)] * 2,
        scratch_shapes=[pltpu.SemaphoreType.DMA((2, PIECES))],
        compiler_params=pltpu.CompilerParams(vmem_limit_bytes=8 * 1024 * 1024),
        cost_estimate=pl.CostEstimate(flops=0, bytes_accessed=4 * 2**20, transcendentals=0),
        name="store",
    )(*[pltpu.with_memory_space_constraint(array, pltpu.VMEM) for array in (deriv, new)])


def local(rho, incr, accum, ham, modes, coeff, damping, links, bath, kinds):
    deriv, new = section(
        rho.reshape(MATS, ROWS, N), incr.reshape(MATS, ROWS, N), accum, ham, modes, coeff, damping,
        links.T, bath.T, kinds.T,
    )
    return store(deriv, new)


def solution(mesh):
    in_specs = (
        P("hier", None, "row", None),
        P("hier", None, "row", None),
        P("hier", None, "row", None),
        P("row", None),
        P(),
        P(),
        P("hier"),
        P(),
        P(),
        P(),
    )
    out_specs = (P("hier", None, "row", None), P("hier", None, "row", None))
    return jax.shard_map(local, mesh=mesh, in_specs=in_specs, out_specs=out_specs, check_vma=False)
```

```python
import jax
import jax.numpy as jnp
from jax import lax
from jax.experimental import pallas as pl
from jax.experimental.pallas import tpu as pltpu
from jax.sharding import PartitionSpec as P

half_step = 0.1
third_step = 0.2 / 3.0

MESH = pl.DeviceIdType.MESH
GROUPS = 4
ZS = 8
YS = 4
YC = 8
OWN = 16
CAP = 4
MATS = 32
ROWS = 16
N = 1024
BATH = 8
SLOTS = 4
CHUNKS = 4
WIDE = N // CHUNKS
HALF = WIDE // 2
QUART = N // GROUPS
TILE = 256
PIECES = 1
LOW = 4
SPLIT = 4


def split(x):
    hi = x.astype(jnp.bfloat16)
    return hi, (x - hi.astype(jnp.float32)).astype(jnp.bfloat16)


def dot(a, b):
    return jnp.dot(a, b, preferred_element_type=jnp.float32)


def sorted_links(links_vec, rows_of, target):
    block = links_vec[...]
    member = lax.broadcasted_iota(jnp.int32, block.shape, 1) - rows_of * OWN
    mine = (member >= 0) & (member < OWN)
    low = target * OWN
    found, last = [], low - 1
    for _ in range(CAP):
        inside = mine & (block > last) & (block < low + OWN)
        last = jnp.minimum(jnp.min(jnp.where(inside, block, low + OWN - 1)), low + OWN - 1)
        found.append(last)
    return found


def kernel(
    rho, incr, accum, ham_hbm, modes_hbm, coeff_hbm, damping_hbm, links_hbm, bath_hbm, kinds_hbm,
    acc, new,
    ham, modes, coeff, damping, links_vec, links, bath, kinds,
    panels, rho_buf, incr_buf, ham_buf, ham_hi, ham_lo, z_in, y_in, right_cat, left, y_back, z_back,
    pool, picked, gap, total,
    line_sem, across_sem, rho_sem, incr_sem, load_sem, h1_send, h1_recv, h2_send, h2_recv, h3_send, h3_recv, h4_send, h4_recv,
    zi_send, zi_recv, yi_send, yi_recv, yb_send, yb_recv, zb_send, zb_recv, pick_send, pick_recv,
):
    h = lax.axis_index("hier")
    r = lax.axis_index("row")
    z = r // YC
    yc = r % YC
    y = yc // 2
    c = yc % 2

    def remote(src, dst, send, recv, group, row):
        return pltpu.make_async_remote_copy(
            src_ref=src, dst_ref=dst, send_sem=send, recv_sem=recv,
            device_id=(group, row), device_id_type=MESH,
        )

    def wait_bytes(ref, sem):
        pltpu.make_async_copy(ref, ref, sem).wait()

    def other_z(k):
        there = (z + ZS // 2 + k // 2 * (2 * (k % 2) - 1) + ZS) % ZS
        return there, there * YC + yc

    def other_yc(k):
        there = (yc + k) % YC
        return there, z * YC + there

    def each(first, last, body):
        def step(k, carry):
            body(k)
            return carry

        lax.fori_loop(first, last, step, 0)

    def load_panel(j):
        part = (slice(None), slice(None), pl.ds(j * WIDE, WIDE))
        return (
            pltpu.make_async_copy(rho.at[part], rho_buf.at[part], rho_sem.at[j]),
            pltpu.make_async_copy(incr.at[part], incr_buf.at[part], incr_sem.at[j]),
        )

    pairs = [
        (ham_hbm, ham), (modes_hbm, modes), (coeff_hbm, coeff), (damping_hbm, damping), (links_hbm, links_vec),
        (links_hbm, links), (bath_hbm, bath), (kinds_hbm, kinds), (accum, new),
    ]
    loads = [pltpu.make_async_copy(src, dst, load_sem.at[i]) for i, (src, dst) in enumerate(pairs)]
    barrier = pltpu.get_barrier_semaphore()

    def greet(group, row):
        pl.semaphore_signal(barrier, inc=1, device_id=(group, row), device_id_type=MESH)

    def across(body):
        each(1, YC, lambda k: body(h, other_yc(k)[1]))
        each(1, GROUPS, lambda k: body((h + k) % GROUPS, r))

    each(1, ZS, lambda k: greet(h, other_z(k)[1]))
    loads[0].start()
    for load in load_panel(0):
        load.start()

    @pl.when(z == 0)
    def _():
        across(greet)


    def make_panels(j):
        for load in load_panel(j):
            load.wait()
        cols = pl.ds(j * WIDE, WIDE)

        def make(m):
            part = pl.ds(m * 8, 8)
            panels[part, :, cols] = rho_buf[part, :, cols] + half_step * incr_buf[part, :, cols]

        each(0, MATS // 8, make)

    loads[0].wait()

    @pl.when(z == 0)
    def _():
        pl.semaphore_wait(barrier, ZS - 1 + YC - 1 + GROUPS - 1)

    @pl.when(z != 0)
    def _():
        pl.semaphore_wait(barrier, ZS - 1)


    ham_own = ham.at[:, pl.ds(pl.multiple_of(h * QUART, QUART), QUART)]

    turn = 1 - 2 * c

    def ham_along(source, part, offset, sem):
        dst = ham_buf.at[h, c, source, y]
        remote(part, dst, h1_send, h1_recv.at[sem], h, (z + offset * turn + ZS) % ZS * YC + yc).start()

    pltpu.make_async_copy(ham_own, ham_buf.at[h, c, z, y], h1_recv.at[2]).start()
    ham_along(z, ham_own, 2, 0)
    ham_along(z, ham_own, -2, 1)
    ham_along(z, ham_own, 1, 2)
    ham_along(z, ham_own, -1, 2)

    def start_chunk(j, first=1, last=ZS):
        cols = pl.ds(j * WIDE, WIDE)

        def send_z(k):
            there, row = other_z(k)
            remote(
                panels.at[pl.ds(there * YS, YS), :, cols], z_in.at[j, z], zi_send.at[j], zi_recv.at[j], h, row
            ).start()

        if first == 1:
            make_panels(j)
            pltpu.make_async_copy(panels.at[pl.ds(z * YS, YS), :, cols], z_in.at[j, z], zi_recv.at[j]).start()
        each(first, last, send_z)

    start_chunk(0, 1, SPLIT)

    def signal(sem, group, row):
        pl.semaphore_signal(sem, inc=1, device_id=(group, row), device_id_type=MESH)

    @pl.when(z == 0)
    def _():
        across(lambda group, row: signal(line_sem, group, row))

    for j in range(1, CHUNKS):
        for load in load_panel(j):
            load.start()
    for load in loads[1:]:
        load.start()

    before, behind = (z + ZS - 2 * turn) % ZS, (z + ZS + 2 * turn) % ZS
    wait_bytes(ham_buf.at[h, c, before, y], h1_recv.at[0])
    wait_bytes(ham_buf.at[h, c, behind, y], h1_recv.at[1])
    ham_along(before, ham_buf.at[h, c, before, y], 1, 2)
    ham_along(behind, ham_buf.at[h, c, behind, y], -1, 2)
    ham_along(before, ham_buf.at[h, c, before, y], 2, 2)

    start_chunk(0, SPLIT, ZS)
    for j in range(1, CHUNKS):
        start_chunk(j)

    @pl.when(z == 0)
    def _():
        pl.semaphore_wait(line_sem, YC - 1 + GROUPS - 1)
        each(1, ZS, lambda k: signal(across_sem, h, other_z(k)[1]))

    @pl.when(z != 0)
    def _():
        pl.semaphore_wait(across_sem, 1)

    wait_bytes(ham_buf.at[h, c, pl.ds(0, ZS - 2), y], h1_recv.at[2])
    low, high = pl.ds(0, LOW), pl.ds(LOW, ZS - LOW)

    def y_row(k):
        return z * YC + (y + k) % YS * 2 + c

    for k in (1, 3, 2):
        part = ham_buf.at[h, c, low, y]
        remote(part, part, h2_send.at[0], h2_recv.at[0], h, y_row(k)).start()
        part = ham_buf.at[h, c, high, y]
        remote(part, part, h2_send.at[1], h2_recv.at[1], (h + k) % GROUPS, r).start()

    def low_on(y_from):
        part = ham_buf.at[h, c, low, y_from]
        for k in (1, 3, 2):
            remote(part, part, h3_send.at[k - 1], h3_recv.at[k - 1], (h + k) % GROUPS, r).start()

    def high_on(group):
        part = ham_buf.at[group, c, high, y]
        for k in (1, 3, 2):
            remote(part, part, h3_send.at[k + 2], h3_recv.at[k + 2], h, y_row(k)).start()

    low_on(y)
    high_on(h)
    for load in loads[1:]:
        load.wait()

    for d in range(1, GROUPS):
        chosen = sorted_links(links_vec, (h + d) % GROUPS, h)
        for i in range(CAP):
            place = (chosen[i] - h * OWN) * 2
            picked[d - 1, 2 * i] = panels[place]
            picked[d - 1, 2 * i + 1] = panels[place + 1]

    def low_part(k, core):
        return ham_buf.at[(h + GROUPS - k) % GROUPS, core, low]

    def high_part(k, core):
        return ham_buf.at[:, core, high, (y + YS - k) % YS]

    def to_core(part, i):
        remote(part, part, h4_send.at[i], h4_recv.at[i], h, r - c + 1 - c).start()

    wait_bytes(ham_buf.at[h, c, low, pl.ds(0, YS - 1)], h2_recv.at[0])
    for k in (1, 3, 2):
        low_on((y + k) % YS)
    wait_bytes(ham_buf.at[pl.ds(0, GROUPS - 1), c, high, y], h2_recv.at[1])
    for k in (1, 3, 2):
        high_on((h + k) % GROUPS)
    to_core(low_part(0, c), 0)
    to_core(high_part(0, c), GROUPS)

    def forward_in(j):
        wait_bytes(z_in.at[j], zi_recv.at[j])

        def send_y(k):
            there, row = other_yc(k)
            remote(
                z_in.at[j, :, there // 2, :, pl.ds(pl.multiple_of(there % 2 * HALF, HALF), HALF)],
                y_in.at[j, :, yc], yi_send.at[j], yi_recv.at[j], h, row,
            ).start()

        pltpu.make_async_copy(
            z_in.at[j, :, y, :, pl.ds(pl.multiple_of(c * HALF, HALF), HALF)], y_in.at[j, :, yc], yi_recv.at[j]
        ).start()
        each(1, YC, send_y)

    def take(q, k):
        cols = pl.ds(pl.multiple_of(q * QUART, QUART), QUART)
        for cc in range(2):
            hi, lo = split(ham_buf[q, cc, k // YS, k % YS])
            rows = pl.ds(pl.multiple_of((k * 2 + cc) * ROWS, ROWS), ROWS)
            ham_hi[rows, cols] = hi
            ham_lo[rows, cols] = lo

    def take_low(k):
        wait_bytes(low_part(k, 1 - c), h4_recv.at[k])
        q = (h + GROUPS - k) % GROUPS
        each(0, LOW * YS, lambda i: take(q, i))

    def take_high(k):
        wait_bytes(high_part(k, 1 - c), h4_recv.at[GROUPS + k])
        yy = (y + YS - k) % YS
        each(0, (ZS - LOW) * GROUPS, lambda i: take(i // (ZS - LOW), (LOW + i % (ZS - LOW)) * YS + yy))

    def multiply_left(j):
        wait_bytes(y_in.at[j], yi_recv.at[j])

        def cut(k):
            hi, lo = split(y_in[j, k].reshape(YC * ROWS, HALF))
            rows = pl.ds(pl.multiple_of(k * YC * ROWS, YC * ROWS), YC * ROWS)
            right_cat[rows, 0:HALF] = hi
            right_cat[rows, HALF:WIDE] = lo

        each(0, ZS, cut)

        def half(i):
            def rows_of(ref):
                starts = [(z + 2 + i * (ZS // 2) + k) % ZS * (YC * ROWS) for k in range(ZS // 2)]
                return jnp.concatenate([ref[pl.ds(pl.multiple_of(at, YC * ROWS), YC * ROWS), :] for at in starts], axis=0)

            both = dot(rows_of(ham_hi), right_cat[...])
            value = both[:, HALF:] + dot(rows_of(ham_lo), right_cat[:, 0:HALF]) + both[:, :HALF]
            part = pl.ds(i * (ZS // 2), ZS // 2)
            left[j, part] = value.reshape(ZS // 2, YC, ROWS, HALF)
            dst = y_back.at[j, part, y, :, pl.ds(pl.multiple_of(c * HALF, HALF), HALF)]

            def send_y(k):
                there, row = other_yc(k)
                remote(left.at[j, part, there], dst, yb_send.at[j], yb_recv.at[j, i], h, row).start()

            pltpu.make_async_copy(left.at[j, part, yc], dst, yb_recv.at[j, i]).start()
            each(1, YC, send_y)

        each(0, 2, half)

    def forward_back(j):
        def send_z(place):
            there = (z + 2 + place) % ZS
            remote(
                y_back.at[j, place], z_back.at[j, pl.ds(z * YS, YS)], zb_send.at[j], zb_recv.at[j], h,
                there * YC + yc,
            ).start()

        wait_bytes(y_back.at[j, pl.ds(0, ZS // 2)], yb_recv.at[j, 0])
        for place in (2, 1, 3, 0):
            send_z(place)
        wait_bytes(y_back.at[j, pl.ds(ZS // 2, ZS // 2)], yb_recv.at[j, 1])
        pltpu.make_async_copy(y_back.at[j, ZS - 2], z_back.at[j, pl.ds(z * YS, YS)], zb_recv.at[j]).start()
        for place in (4, 7, 5):
            send_z(place)

    def multiply_right(k):
        rows = pl.ds(k * (TILE // ROWS), TILE // ROWS)
        hi, lo = split(panels[rows].reshape(TILE, N))

        def columns(q):
            cols = pl.ds(pl.multiple_of(q * TILE, TILE), TILE)
            top = ham_hi[:, cols]
            value = dot(hi, ham_lo[:, cols]) + dot(lo, top) + dot(hi, top)
            value = value.reshape(TILE // ROWS // 2, 2, ROWS, TILE)
            pairs = pl.ds(k * (TILE // ROWS // 2), TILE // ROWS // 2)
            acc[pairs, 0, :, cols] = acc[pairs, 0, :, cols] - value[:, 1]
            acc[pairs, 1, :, cols] = acc[pairs, 1, :, cols] + value[:, 0]

        each(0, N // TILE, columns)

    def decay(a):
        rate = damping[a]
        first, second = panels[2 * a], panels[2 * a + 1]
        acc[a, 0] = -(rate * first)
        acc[a, 1] = -(rate * second)
        pool[2 * a] = first
        pool[2 * a + 1] = second

    each(0, OWN, decay)

    lane = lax.broadcasted_iota(jnp.int32, (ROWS, N), 1)
    diagonal = lane == lax.broadcasted_iota(jnp.int32, (ROWS, N), 0) + r * ROWS
    for k in range(BATH):
        columns = jnp.broadcast_to(modes[k : k + 1, :], (ROWS, N))
        row_part = jnp.sum(jnp.where(diagonal, columns, 0.0), axis=1, keepdims=True)
        gap[k] = row_part - columns
        total[k] = row_part + columns

    forward_in(0)
    take_low(0)
    take_high(0)
    for k in (1, 3, 2):
        wait_bytes(low_part(k, c), h3_recv.at[k - 1])
        to_core(low_part(k, c), k)
        wait_bytes(high_part(k, c), h3_recv.at[k + 2])
        to_core(high_part(k, c), GROUPS + k)
    for k in (1, 2, 3):
        remote(
            picked.at[k - 1], pool.at[pl.ds(MATS + (k - 1) * 2 * CAP, 2 * CAP)],
            pick_send.at[k - 1], pick_recv.at[k - 1], (h + k) % GROUPS, r,
        ).start()
    forward_in(1)
    for k in (1, 3, 2):
        take_low(k)
        take_high(k)
    multiply_left(0)
    multiply_left(1)
    forward_back(0)
    forward_in(2)
    forward_back(1)
    forward_in(3)
    multiply_left(2)
    multiply_left(3)
    forward_back(2)
    forward_back(3)
    each(0, MATS * ROWS // TILE, multiply_right)

    for d in range(1, GROUPS):
        wait_bytes(pool.at[pl.ds(MATS + (d - 1) * 2 * CAP, 2 * CAP)], pick_recv.at[d - 1])
    names = []
    for d in range(1, GROUPS):
        names += sorted_links(links_vec, h, (h + GROUPS - d) % GROUPS)

    def couple(a):
        real, imag = acc[a, 0], acc[a, 1]
        for slot in range(SLOTS):
            link = links[slot, h * OWN + a]
            mode = bath[slot, h * OWN + a]
            kind = kinds[slot, h * OWN + a]
            place = link - h * OWN
            for i, name in enumerate(names):
                place = jnp.where(link == name, OWN + i, place)
            place = jnp.clip(place, 0, OWN + (GROUPS - 1) * CAP - 1)
            direct = jnp.where(kind == 1, 1.0, jnp.where(kind == 2, coeff[0, mode], 0.0))
            mixing = jnp.where(kind == 2, coeff[1, mode], 0.0)
            first, second = pool[2 * place], pool[2 * place + 1]
            across = direct * gap[mode]
            along = mixing * total[mode]
            real = real + (across * second + along * first)
            imag = imag + (along * second - across * first)
        acc[a, 0], acc[a, 1] = real, imag

    each(0, OWN, couple)

    def wait_sent():
        wait_bytes(ham_buf.at[0, 0, pl.ds(0, ZS - 1), 0], h1_send)
        wait_bytes(ham_buf.at[0, 0, low, pl.ds(0, YS - 1)], h2_send.at[0])
        wait_bytes(ham_buf.at[0, 0, high, pl.ds(0, YS - 1)], h2_send.at[1])
        for k in range(GROUPS - 1):
            wait_bytes(low_part(0, 0), h3_send.at[k])
            wait_bytes(high_part(0, 0), h3_send.at[GROUPS - 1 + k])
        for k in range(GROUPS):
            wait_bytes(low_part(0, 0), h4_send.at[k])
            wait_bytes(high_part(0, 0), h4_send.at[GROUPS + k])
        for k in range(GROUPS - 1):
            wait_bytes(picked.at[0], pick_send.at[k])
        for j in range(CHUNKS):
            wait_bytes(z_in.at[0, pl.ds(0, ZS - 1)], zi_send.at[j])
            wait_bytes(y_in.at[0, :, pl.ds(0, YC - 1)], yi_send.at[j])
            wait_bytes(left.at[0, :, pl.ds(0, YC - 1)], yb_send.at[j])
            if j < CHUNKS - 1:
                wait_bytes(y_back.at[0, pl.ds(0, ZS - 1)], zb_send.at[j])

    for j in range(CHUNKS):
        cols = pl.ds(j * WIDE, WIDE)
        if j == CHUNKS - 1:
            wait_sent()
        wait_bytes(z_back.at[j], zb_recv.at[j])

        def finish(k, j=j, cols=cols):
            part = pl.ds(k * 2, 2)
            back = z_back[j, pl.ds(k * 4, 4)].reshape(2, 2, ROWS, WIDE)
            real = acc[part, 0, :, cols] + back[:, 1]
            imag = acc[part, 1, :, cols] - back[:, 0]
            acc[part, 0, :, cols] = real
            acc[part, 1, :, cols] = imag
            new[part, 0, :, cols] = new[part, 0, :, cols] + third_step * real
            new[part, 1, :, cols] = new[part, 1, :, cols] + third_step * imag

        each(0, OWN // 2, finish)

    wait_bytes(y_back.at[0, pl.ds(0, ZS - 1)], zb_send.at[CHUNKS - 1])


def section(*arrays):
    f32, bf16, i32 = jnp.float32, jnp.bfloat16, jnp.int32
    dma = pltpu.SemaphoreType.DMA
    four = (CHUNKS,)
    outs = [pltpu.VMEM((OWN, 2, ROWS, N), f32)] * 2
    return pl.pallas_call(
        kernel,
        out_shape=outs,
        in_specs=[pl.BlockSpec(memory_space=pltpu.HBM)] * len(arrays),
        out_specs=[pl.BlockSpec(memory_space=pltpu.VMEM)] * 2,
        scratch_shapes=[
            pltpu.VMEM((ROWS, N), f32),
            pltpu.VMEM((BATH, N), f32),
            pltpu.SMEM((2, BATH), f32),
            pltpu.SMEM((OWN,), f32),
            pltpu.VMEM((SLOTS, GROUPS * OWN), i32),
            pltpu.SMEM((SLOTS, GROUPS * OWN), i32),
            pltpu.SMEM((SLOTS, GROUPS * OWN), i32),
            pltpu.SMEM((SLOTS, GROUPS * OWN), i32),
            pltpu.VMEM((MATS, ROWS, N), f32),
            pltpu.VMEM((MATS, ROWS, N), f32),
            pltpu.VMEM((MATS, ROWS, N), f32),
            pltpu.VMEM((GROUPS, 2, ZS, YS, ROWS, QUART), f32),
            pltpu.VMEM((N, N), bf16),
            pltpu.VMEM((N, N), bf16),
            pltpu.VMEM((CHUNKS, ZS, YS, ROWS, WIDE), f32),
            pltpu.VMEM((CHUNKS, ZS, YC, ROWS, HALF), f32),
            pltpu.VMEM((N, WIDE), bf16),
            pltpu.VMEM((CHUNKS, ZS, YC, ROWS, HALF), f32),
            pltpu.VMEM((CHUNKS, ZS, YS, ROWS, WIDE), f32),
            pltpu.VMEM((CHUNKS, MATS, ROWS, WIDE), f32),
            pltpu.VMEM((MATS + (GROUPS - 1) * 2 * CAP, ROWS, N), f32),
            pltpu.VMEM((GROUPS - 1, 2 * CAP, ROWS, N), f32),
            pltpu.VMEM((BATH, ROWS, N), f32),
            pltpu.VMEM((BATH, ROWS, N), f32),
            pltpu.SemaphoreType.REGULAR, pltpu.SemaphoreType.REGULAR,
            dma(four), dma(four), dma((9,)),
            dma, dma((3,)), dma((2,)), dma((2,)),
            dma((6,)), dma((6,)), dma((8,)), dma((8,)),
            dma(four), dma(four), dma(four), dma(four),
            dma(four), dma((CHUNKS, 2)), dma(four), dma(four),
            dma((3,)), dma((3,)),
        ],
        compiler_params=pltpu.CompilerParams(
            collective_id=0, has_side_effects=True, vmem_limit_bytes=48 * 1024 * 1024
        ),
        cost_estimate=pl.CostEstimate(flops=6 * 2**30, bytes_accessed=6 * 2**20, transcendentals=0),
        name="section",
    )(*[pltpu.with_memory_space_constraint(array, pltpu.HBM) for array in arrays])


def store_kernel(deriv, new, deriv_out, new_out, sem):
    copies = []
    for i in range(PIECES):
        part = pl.ds(i * (OWN // PIECES), OWN // PIECES)
        copies.append(pltpu.make_async_copy(deriv.at[part], deriv_out.at[part], sem.at[0, i]))
        copies.append(pltpu.make_async_copy(new.at[part], new_out.at[part], sem.at[1, i]))
    for copy in copies:
        copy.start()
    for copy in copies:
        copy.wait()


def store(deriv, new):
    shape = jax.ShapeDtypeStruct(deriv.shape, deriv.dtype)
    return pl.pallas_call(
        store_kernel,
        out_shape=[shape] * 2,
        in_specs=[pl.BlockSpec(memory_space=pltpu.VMEM)] * 2,
        out_specs=[pl.BlockSpec(memory_space=pltpu.HBM)] * 2,
        scratch_shapes=[pltpu.SemaphoreType.DMA((2, PIECES))],
        compiler_params=pltpu.CompilerParams(vmem_limit_bytes=8 * 1024 * 1024),
        cost_estimate=pl.CostEstimate(flops=0, bytes_accessed=4 * 2**20, transcendentals=0),
        name="store",
    )(*[pltpu.with_memory_space_constraint(array, pltpu.VMEM) for array in (deriv, new)])


def local(rho, incr, accum, ham, modes, coeff, damping, links, bath, kinds):
    deriv, new = section(
        rho.reshape(MATS, ROWS, N), incr.reshape(MATS, ROWS, N), accum, ham, modes, coeff, damping,
        links.T, bath.T, kinds.T,
    )
    return store(deriv, new)


def solution(mesh):
    in_specs = (
        P("hier", None, "row", None),
        P("hier", None, "row", None),
        P("hier", None, "row", None),
        P("row", None),
        P(),
        P(),
        P("hier"),
        P(),
        P(),
        P(),
    )
    out_specs = (P("hier", None, "row", None), P("hier", None, "row", None))
    return jax.shard_map(local, mesh=mesh, in_specs=in_specs, out_specs=out_specs, check_vma=False)
```

```python
import jax
import jax.numpy as jnp
from jax import lax
from jax.experimental import pallas as pl
from jax.experimental.pallas import tpu as pltpu
from jax.sharding import PartitionSpec as P

half_step = 0.1
third_step = 0.2 / 3.0

MESH = pl.DeviceIdType.MESH
GROUPS = 4
ZS = 8
YS = 4
YC = 8
OWN = 16
CAP = 4
MATS = 32
ROWS = 16
N = 1024
BATH = 8
SLOTS = 4
CHUNKS = 4
WIDE = N // CHUNKS
HALF = WIDE // 2
QUART = N // GROUPS
TILE = 256
PIECES = 4
LOW = 4
SPLIT = 4


def split(x):
    hi = x.astype(jnp.bfloat16)
    return hi, (x - hi.astype(jnp.float32)).astype(jnp.bfloat16)


def dot(a, b):
    return jnp.dot(a, b, preferred_element_type=jnp.float32)


def sorted_links(links_vec, rows_of, target):
    block = links_vec[...]
    member = lax.broadcasted_iota(jnp.int32, block.shape, 1) - rows_of * OWN
    mine = (member >= 0) & (member < OWN)
    low = target * OWN
    found, last = [], low - 1
    for _ in range(CAP):
        inside = mine & (block > last) & (block < low + OWN)
        last = jnp.minimum(jnp.min(jnp.where(inside, block, low + OWN - 1)), low + OWN - 1)
        found.append(last)
    return found


def kernel(
    rho, incr, accum, ham_hbm, modes_hbm, coeff_hbm, damping_hbm, links_hbm, bath_hbm, kinds_hbm,
    acc, new,
    ham, modes, coeff, damping, links_vec, links, bath, kinds,
    panels, rho_buf, incr_buf, ham_buf, ham_hi, ham_lo, z_in, y_in, right_cat, left, y_back, z_back,
    pool, picked, gap, total,
    line_sem, across_sem, rho_sem, incr_sem, load_sem, h1_send, h1_recv, h2_send, h2_recv, h3_send, h3_recv, h4_send, h4_recv,
    zi_send, zi_recv, yi_send, yi_recv, yb_send, yb_recv, zb_send, zb_recv, pick_send, pick_recv,
):
    h = lax.axis_index("hier")
    r = lax.axis_index("row")
    z = r // YC
    yc = r % YC
    y = yc // 2
    c = yc % 2

    def remote(src, dst, send, recv, group, row):
        return pltpu.make_async_remote_copy(
            src_ref=src, dst_ref=dst, send_sem=send, recv_sem=recv,
            device_id=(group, row), device_id_type=MESH,
        )

    def wait_bytes(ref, sem):
        pltpu.make_async_copy(ref, ref, sem).wait()

    def other_z(k):
        there = (z + ZS // 2 + k // 2 * (2 * (k % 2) - 1) * (1 - 2 * c) + ZS) % ZS
        return there, there * YC + yc

    def other_yc(k):
        there = (yc + k) % YC
        return there, z * YC + there

    def each(first, last, body):
        def step(k, carry):
            body(k)
            return carry

        lax.fori_loop(first, last, step, 0)

    def load_panel(j):
        part = (slice(None), slice(None), pl.ds(j * WIDE, WIDE))
        return (
            pltpu.make_async_copy(rho.at[part], rho_buf.at[part], rho_sem.at[j]),
            pltpu.make_async_copy(incr.at[part], incr_buf.at[part], incr_sem.at[j]),
        )

    pairs = [
        (ham_hbm, ham), (modes_hbm, modes), (coeff_hbm, coeff), (damping_hbm, damping), (links_hbm, links_vec),
        (links_hbm, links), (bath_hbm, bath), (kinds_hbm, kinds), (accum, new),
    ]
    loads = [pltpu.make_async_copy(src, dst, load_sem.at[i]) for i, (src, dst) in enumerate(pairs)]
    barrier = pltpu.get_barrier_semaphore()

    def greet(group, row):
        pl.semaphore_signal(barrier, inc=1, device_id=(group, row), device_id_type=MESH)

    def across(body):
        each(1, YC, lambda k: body(h, other_yc(k)[1]))
        each(1, GROUPS, lambda k: body((h + k) % GROUPS, r))

    each(1, ZS, lambda k: greet(h, other_z(k)[1]))
    loads[0].start()
    for load in load_panel(0):
        load.start()

    @pl.when(z == 0)
    def _():
        across(greet)


    def make_panels(j):
        for load in load_panel(j):
            load.wait()
        cols = pl.ds(j * WIDE, WIDE)

        def make(m):
            part = pl.ds(m * 8, 8)
            panels[part, :, cols] = rho_buf[part, :, cols] + half_step * incr_buf[part, :, cols]

        each(0, MATS // 8, make)

    loads[0].wait()

    @pl.when(z == 0)
    def _():
        pl.semaphore_wait(barrier, ZS - 1 + YC - 1 + GROUPS - 1)

    @pl.when(z != 0)
    def _():
        pl.semaphore_wait(barrier, ZS - 1)


    ham_own = ham.at[:, pl.ds(pl.multiple_of(h * QUART, QUART), QUART)]

    turn = 1 - 2 * c

    def ham_along(source, part, offset, sem):
        dst = ham_buf.at[h, c, source, y]
        remote(part, dst, h1_send, h1_recv.at[sem], h, (z + offset * turn + ZS) % ZS * YC + yc).start()

    pltpu.make_async_copy(ham_own, ham_buf.at[h, c, z, y], h1_recv.at[2]).start()
    ham_along(z, ham_own, 2, 0)
    ham_along(z, ham_own, -2, 1)
    ham_along(z, ham_own, 1, 2)
    ham_along(z, ham_own, -1, 2)

    def start_chunk(j, first=1, last=ZS):
        cols = pl.ds(j * WIDE, WIDE)

        def send_z(k):
            there, row = other_z(k)
            remote(
                panels.at[pl.ds(there * YS, YS), :, cols], z_in.at[j, z], zi_send.at[j], zi_recv.at[j], h, row
            ).start()

        if first == 1:
            make_panels(j)
            pltpu.make_async_copy(panels.at[pl.ds(z * YS, YS), :, cols], z_in.at[j, z], zi_recv.at[j]).start()
        each(first, last, send_z)

    start_chunk(0, 1, SPLIT)

    def signal(sem, group, row):
        pl.semaphore_signal(sem, inc=1, device_id=(group, row), device_id_type=MESH)

    @pl.when(z == 0)
    def _():
        across(lambda group, row: signal(line_sem, group, row))

    for j in range(1, CHUNKS):
        for load in load_panel(j):
            load.start()
    for load in loads[1:]:
        load.start()

    before, behind = (z + ZS - 2 * turn) % ZS, (z + ZS + 2 * turn) % ZS
    wait_bytes(ham_buf.at[h, c, before, y], h1_recv.at[0])
    wait_bytes(ham_buf.at[h, c, behind, y], h1_recv.at[1])
    ham_along(before, ham_buf.at[h, c, before, y], 1, 2)
    ham_along(behind, ham_buf.at[h, c, behind, y], -1, 2)
    ham_along(before, ham_buf.at[h, c, before, y], 2, 2)

    start_chunk(0, SPLIT, ZS)
    for j in range(1, CHUNKS):
        start_chunk(j)

    @pl.when(z == 0)
    def _():
        pl.semaphore_wait(line_sem, YC - 1 + GROUPS - 1)
        each(1, ZS, lambda k: signal(across_sem, h, other_z(k)[1]))

    @pl.when(z != 0)
    def _():
        pl.semaphore_wait(across_sem, 1)

    wait_bytes(ham_buf.at[h, c, pl.ds(0, ZS - 2), y], h1_recv.at[2])
    low, high = pl.ds(0, LOW), pl.ds(LOW, ZS - LOW)

    def y_row(k):
        return z * YC + (y + k) % YS * 2 + c

    for k in (1, 3, 2):
        part = ham_buf.at[h, c, low, y]
        remote(part, part, h2_send.at[0], h2_recv.at[0], h, y_row(k)).start()
        part = ham_buf.at[h, c, high, y]
        remote(part, part, h2_send.at[1], h2_recv.at[1], (h + k) % GROUPS, r).start()

    def low_on(y_from):
        part = ham_buf.at[h, c, low, y_from]
        for k in (1, 3, 2):
            remote(part, part, h3_send.at[k - 1], h3_recv.at[k - 1], (h + k) % GROUPS, r).start()

    def high_on(group):
        part = ham_buf.at[group, c, high, y]
        for k in (1, 3, 2):
            remote(part, part, h3_send.at[k + 2], h3_recv.at[k + 2], h, y_row(k)).start()

    low_on(y)
    high_on(h)
    for load in loads[1:]:
        load.wait()

    for d in range(1, GROUPS):
        chosen = sorted_links(links_vec, (h + d) % GROUPS, h)
        for i in range(CAP):
            place = (chosen[i] - h * OWN) * 2
            picked[d - 1, 2 * i] = panels[place]
            picked[d - 1, 2 * i + 1] = panels[place + 1]

    def low_part(k, core):
        return ham_buf.at[(h + GROUPS - k) % GROUPS, core, low]

    def high_part(k, core):
        return ham_buf.at[:, core, high, (y + YS - k) % YS]

    def to_core(part, i):
        remote(part, part, h4_send.at[i], h4_recv.at[i], h, r - c + 1 - c).start()

    wait_bytes(ham_buf.at[h, c, low, pl.ds(0, YS - 1)], h2_recv.at[0])
    for k in (1, 3, 2):
        low_on((y + k) % YS)
    wait_bytes(ham_buf.at[pl.ds(0, GROUPS - 1), c, high, y], h2_recv.at[1])
    for k in (1, 3, 2):
        high_on((h + k) % GROUPS)
    to_core(low_part(0, c), 0)
    to_core(high_part(0, c), GROUPS)

    def forward_in(j):
        wait_bytes(z_in.at[j], zi_recv.at[j])

        def send_y(k):
            there, row = other_yc(k)
            remote(
                z_in.at[j, :, there // 2, :, pl.ds(pl.multiple_of(there % 2 * HALF, HALF), HALF)],
                y_in.at[j, :, yc], yi_send.at[j], yi_recv.at[j], h, row,
            ).start()

        pltpu.make_async_copy(
            z_in.at[j, :, y, :, pl.ds(pl.multiple_of(c * HALF, HALF), HALF)], y_in.at[j, :, yc], yi_recv.at[j]
        ).start()
        each(1, YC, send_y)

    def take(q, k):
        cols = pl.ds(pl.multiple_of(q * QUART, QUART), QUART)
        for cc in range(2):
            hi, lo = split(ham_buf[q, cc, k // YS, k % YS])
            rows = pl.ds(pl.multiple_of((k * 2 + cc) * ROWS, ROWS), ROWS)
            ham_hi[rows, cols] = hi
            ham_lo[rows, cols] = lo

    def take_low(k):
        wait_bytes(low_part(k, 1 - c), h4_recv.at[k])
        q = (h + GROUPS - k) % GROUPS
        each(0, LOW * YS, lambda i: take(q, i))

    def take_high(k):
        wait_bytes(high_part(k, 1 - c), h4_recv.at[GROUPS + k])
        yy = (y + YS - k) % YS
        each(0, (ZS - LOW) * GROUPS, lambda i: take(i // (ZS - LOW), (LOW + i % (ZS - LOW)) * YS + yy))

    def multiply_left(j):
        wait_bytes(y_in.at[j], yi_recv.at[j])

        def cut(k):
            hi, lo = split(y_in[j, k].reshape(YC * ROWS, HALF))
            rows = pl.ds(pl.multiple_of(k * YC * ROWS, YC * ROWS), YC * ROWS)
            right_cat[rows, 0:HALF] = hi
            right_cat[rows, HALF:WIDE] = lo

        each(0, ZS, cut)

        def half(i):
            def rows_of(ref):
                starts = [(z + 2 + i * (ZS // 2) + k) % ZS * (YC * ROWS) for k in range(ZS // 2)]
                return jnp.concatenate([ref[pl.ds(pl.multiple_of(at, YC * ROWS), YC * ROWS), :] for at in starts], axis=0)

            both = dot(rows_of(ham_hi), right_cat[...])
            value = both[:, HALF:] + dot(rows_of(ham_lo), right_cat[:, 0:HALF]) + both[:, :HALF]
            part = pl.ds(i * (ZS // 2), ZS // 2)
            left[j, part] = value.reshape(ZS // 2, YC, ROWS, HALF)
            dst = y_back.at[j, part, y, :, pl.ds(pl.multiple_of(c * HALF, HALF), HALF)]

            def send_y(k):
                there, row = other_yc(k)
                remote(left.at[j, part, there], dst, yb_send.at[j], yb_recv.at[j, i], h, row).start()

            pltpu.make_async_copy(left.at[j, part, yc], dst, yb_recv.at[j, i]).start()
            each(1, YC, send_y)

        each(0, 2, half)

    def forward_back(j):
        def send_z(place):
            there = (z + 2 + place) % ZS
            remote(
                y_back.at[j, place], z_back.at[j, pl.ds(z * YS, YS)], zb_send.at[j], zb_recv.at[j], h,
                there * YC + yc,
            ).start()

        wait_bytes(y_back.at[j, pl.ds(0, ZS // 2)], yb_recv.at[j, 0])
        for place in (2, 1, 3, 0):
            send_z(place)
        wait_bytes(y_back.at[j, pl.ds(ZS // 2, ZS // 2)], yb_recv.at[j, 1])
        pltpu.make_async_copy(y_back.at[j, ZS - 2], z_back.at[j, pl.ds(z * YS, YS)], zb_recv.at[j]).start()
        for place in (4, 7, 5):
            send_z(place)

    def multiply_right(k):
        rows = pl.ds(k * (TILE // ROWS), TILE // ROWS)
        hi, lo = split(panels[rows].reshape(TILE, N))

        def columns(q):
            cols = pl.ds(pl.multiple_of(q * TILE, TILE), TILE)
            top = ham_hi[:, cols]
            value = dot(hi, ham_lo[:, cols]) + dot(lo, top) + dot(hi, top)
            value = value.reshape(TILE // ROWS // 2, 2, ROWS, TILE)
            pairs = pl.ds(k * (TILE // ROWS // 2), TILE // ROWS // 2)
            acc[pairs, 0, :, cols] = acc[pairs, 0, :, cols] - value[:, 1]
            acc[pairs, 1, :, cols] = acc[pairs, 1, :, cols] + value[:, 0]

        each(0, N // TILE, columns)

    def decay(a):
        rate = damping[a]
        first, second = panels[2 * a], panels[2 * a + 1]
        acc[a, 0] = -(rate * first)
        acc[a, 1] = -(rate * second)
        pool[2 * a] = first
        pool[2 * a + 1] = second

    each(0, OWN, decay)

    lane = lax.broadcasted_iota(jnp.int32, (ROWS, N), 1)
    diagonal = lane == lax.broadcasted_iota(jnp.int32, (ROWS, N), 0) + r * ROWS
    for k in range(BATH):
        columns = jnp.broadcast_to(modes[k : k + 1, :], (ROWS, N))
        row_part = jnp.sum(jnp.where(diagonal, columns, 0.0), axis=1, keepdims=True)
        gap[k] = row_part - columns
        total[k] = row_part + columns

    forward_in(0)
    take_low(0)
    take_high(0)
    for k in (1, 3, 2):
        wait_bytes(low_part(k, c), h3_recv.at[k - 1])
        to_core(low_part(k, c), k)
        wait_bytes(high_part(k, c), h3_recv.at[k + 2])
        to_core(high_part(k, c), GROUPS + k)
    for k in (1, 2, 3):
        remote(
            picked.at[k - 1], pool.at[pl.ds(MATS + (k - 1) * 2 * CAP, 2 * CAP)],
            pick_send.at[k - 1], pick_recv.at[k - 1], (h + k) % GROUPS, r,
        ).start()
    forward_in(1)
    for k in (1, 3, 2):
        take_low(k)
        take_high(k)
    multiply_left(0)
    multiply_left(1)
    forward_back(0)
    forward_in(2)
    forward_back(1)
    forward_in(3)
    multiply_left(2)
    multiply_left(3)
    forward_back(2)
    forward_back(3)
    each(0, MATS * ROWS // TILE, multiply_right)

    for d in range(1, GROUPS):
        wait_bytes(pool.at[pl.ds(MATS + (d - 1) * 2 * CAP, 2 * CAP)], pick_recv.at[d - 1])
    names = []
    for d in range(1, GROUPS):
        names += sorted_links(links_vec, h, (h + GROUPS - d) % GROUPS)

    def couple(a):
        real, imag = acc[a, 0], acc[a, 1]
        for slot in range(SLOTS):
            link = links[slot, h * OWN + a]
            mode = bath[slot, h * OWN + a]
            kind = kinds[slot, h * OWN + a]
            place = link - h * OWN
            for i, name in enumerate(names):
                place = jnp.where(link == name, OWN + i, place)
            place = jnp.clip(place, 0, OWN + (GROUPS - 1) * CAP - 1)
            direct = jnp.where(kind == 1, 1.0, jnp.where(kind == 2, coeff[0, mode], 0.0))
            mixing = jnp.where(kind == 2, coeff[1, mode], 0.0)
            first, second = pool[2 * place], pool[2 * place + 1]
            across = direct * gap[mode]
            along = mixing * total[mode]
            real = real + (across * second + along * first)
            imag = imag + (along * second - across * first)
        acc[a, 0], acc[a, 1] = real, imag

    each(0, OWN, couple)

    for j in range(CHUNKS):
        cols = pl.ds(j * WIDE, WIDE)
        wait_bytes(z_back.at[j], zb_recv.at[j])

        def finish(k, j=j, cols=cols):
            part = pl.ds(k * 2, 2)
            back = z_back[j, pl.ds(k * 4, 4)].reshape(2, 2, ROWS, WIDE)
            real = acc[part, 0, :, cols] + back[:, 1]
            imag = acc[part, 1, :, cols] - back[:, 0]
            acc[part, 0, :, cols] = real
            acc[part, 1, :, cols] = imag
            new[part, 0, :, cols] = new[part, 0, :, cols] + third_step * real
            new[part, 1, :, cols] = new[part, 1, :, cols] + third_step * imag

        each(0, OWN // 2, finish)

    wait_bytes(ham_buf.at[0, 0, pl.ds(0, ZS - 1), 0], h1_send)
    wait_bytes(ham_buf.at[0, 0, low, pl.ds(0, YS - 1)], h2_send.at[0])
    wait_bytes(ham_buf.at[0, 0, high, pl.ds(0, YS - 1)], h2_send.at[1])
    for k in range(GROUPS - 1):
        wait_bytes(low_part(0, 0), h3_send.at[k])
        wait_bytes(high_part(0, 0), h3_send.at[GROUPS - 1 + k])
    for k in range(GROUPS):
        wait_bytes(low_part(0, 0), h4_send.at[k])
        wait_bytes(high_part(0, 0), h4_send.at[GROUPS + k])
    for k in range(GROUPS - 1):
        wait_bytes(picked.at[0], pick_send.at[k])
    for j in range(CHUNKS):
        wait_bytes(z_in.at[0, pl.ds(0, ZS - 1)], zi_send.at[j])
        wait_bytes(y_in.at[0, :, pl.ds(0, YC - 1)], yi_send.at[j])
        wait_bytes(left.at[0, :, pl.ds(0, YC - 1)], yb_send.at[j])
        wait_bytes(y_back.at[0, pl.ds(0, ZS - 1)], zb_send.at[j])


def section(*arrays):
    f32, bf16, i32 = jnp.float32, jnp.bfloat16, jnp.int32
    dma = pltpu.SemaphoreType.DMA
    four = (CHUNKS,)
    outs = [pltpu.VMEM((OWN, 2, ROWS, N), f32)] * 2
    return pl.pallas_call(
        kernel,
        out_shape=outs,
        in_specs=[pl.BlockSpec(memory_space=pltpu.HBM)] * len(arrays),
        out_specs=[pl.BlockSpec(memory_space=pltpu.VMEM)] * 2,
        scratch_shapes=[
            pltpu.VMEM((ROWS, N), f32),
            pltpu.VMEM((BATH, N), f32),
            pltpu.SMEM((2, BATH), f32),
            pltpu.SMEM((OWN,), f32),
            pltpu.VMEM((SLOTS, GROUPS * OWN), i32),
            pltpu.SMEM((SLOTS, GROUPS * OWN), i32),
            pltpu.SMEM((SLOTS, GROUPS * OWN), i32),
            pltpu.SMEM((SLOTS, GROUPS * OWN), i32),
            pltpu.VMEM((MATS, ROWS, N), f32),
            pltpu.VMEM((MATS, ROWS, N), f32),
            pltpu.VMEM((MATS, ROWS, N), f32),
            pltpu.VMEM((GROUPS, 2, ZS, YS, ROWS, QUART), f32),
            pltpu.VMEM((N, N), bf16),
            pltpu.VMEM((N, N), bf16),
            pltpu.VMEM((CHUNKS, ZS, YS, ROWS, WIDE), f32),
            pltpu.VMEM((CHUNKS, ZS, YC, ROWS, HALF), f32),
            pltpu.VMEM((N, WIDE), bf16),
            pltpu.VMEM((CHUNKS, ZS, YC, ROWS, HALF), f32),
            pltpu.VMEM((CHUNKS, ZS, YS, ROWS, WIDE), f32),
            pltpu.VMEM((CHUNKS, MATS, ROWS, WIDE), f32),
            pltpu.VMEM((MATS + (GROUPS - 1) * 2 * CAP, ROWS, N), f32),
            pltpu.VMEM((GROUPS - 1, 2 * CAP, ROWS, N), f32),
            pltpu.VMEM((BATH, ROWS, N), f32),
            pltpu.VMEM((BATH, ROWS, N), f32),
            pltpu.SemaphoreType.REGULAR, pltpu.SemaphoreType.REGULAR,
            dma(four), dma(four), dma((9,)),
            dma, dma((3,)), dma((2,)), dma((2,)),
            dma((6,)), dma((6,)), dma((8,)), dma((8,)),
            dma(four), dma(four), dma(four), dma(four),
            dma(four), dma((CHUNKS, 2)), dma(four), dma(four),
            dma((3,)), dma((3,)),
        ],
        compiler_params=pltpu.CompilerParams(
            collective_id=0, has_side_effects=True, vmem_limit_bytes=48 * 1024 * 1024
        ),
        cost_estimate=pl.CostEstimate(flops=6 * 2**30, bytes_accessed=6 * 2**20, transcendentals=0),
        name="section",
    )(*[pltpu.with_memory_space_constraint(array, pltpu.HBM) for array in arrays])


def store_kernel(deriv, new, deriv_out, new_out, sem):
    copies = []
    for i in range(PIECES):
        part = pl.ds(i * (OWN // PIECES), OWN // PIECES)
        copies.append(pltpu.make_async_copy(deriv.at[part], deriv_out.at[part], sem.at[0, i]))
        copies.append(pltpu.make_async_copy(new.at[part], new_out.at[part], sem.at[1, i]))
    for copy in copies:
        copy.start()
    for copy in copies:
        copy.wait()


def store(deriv, new):
    shape = jax.ShapeDtypeStruct(deriv.shape, deriv.dtype)
    return pl.pallas_call(
        store_kernel,
        out_shape=[shape] * 2,
        in_specs=[pl.BlockSpec(memory_space=pltpu.VMEM)] * 2,
        out_specs=[pl.BlockSpec(memory_space=pltpu.HBM)] * 2,
        scratch_shapes=[pltpu.SemaphoreType.DMA((2, PIECES))],
        compiler_params=pltpu.CompilerParams(vmem_limit_bytes=8 * 1024 * 1024),
        cost_estimate=pl.CostEstimate(flops=0, bytes_accessed=4 * 2**20, transcendentals=0),
        name="store",
    )(*[pltpu.with_memory_space_constraint(array, pltpu.VMEM) for array in (deriv, new)])


def local(rho, incr, accum, ham, modes, coeff, damping, links, bath, kinds):
    deriv, new = section(
        rho.reshape(MATS, ROWS, N), incr.reshape(MATS, ROWS, N), accum, ham, modes, coeff, damping,
        links.T, bath.T, kinds.T,
    )
    return store(deriv, new)


def solution(mesh):
    in_specs = (
        P("hier", None, "row", None),
        P("hier", None, "row", None),
        P("hier", None, "row", None),
        P("row", None),
        P(),
        P(),
        P("hier"),
        P(),
        P(),
        P(),
    )
    out_specs = (P("hier", None, "row", None), P("hier", None, "row", None))
    return jax.shard_map(local, mesh=mesh, in_specs=in_specs, out_specs=out_specs, check_vma=False)
```
